256 devices in a mesh: row: 8 (over z_hi, y), col: 32 (over x, z_lo, core).
Axes of the slice: x: 4, y: 4, z: 8 (z_hi: 2, z_lo: 4; z = z_hi * 4 + z_lo), core: 2. Of those that a mesh axis runs over, the one named last changes fastest.
Arguments:
- blocks: bfloat16 [256, 8, 8, 256, 256], P('col', 'row'), may hold values from -1.6 to 1.6
- block_cols: int32 [256, 8, 8], P('col', 'row'), may hold values from 0 to 31
- counts: int32 [256, 8], P('col', 'row'), may hold values from 1 to 8, as said below
- random_start_panel: bfloat16 [65536, 128], P(('row', 'col')), may hold values from -6 to 6
Outputs:
- embedding: float32 [65536, 128], P(('row', 'col'))
The draws below stay inside these ranges and needn't reach their ends.
Inputs may be any that keep to these rules, and one draw needn't show every extreme that they name: `counts`: each block row holds 1 to 8 valid slots in each block column range; in every draw some block row holds 8.
All inputs are finite; a program needn't handle non-finite values.
Results may differ from the reference program's by a relative error of at most 0.003.
Values may be sent and summed in bfloat16 or wider, within the bound.
No kernel may reach another device: no remote copies, remote signals or barrier semaphores. Data moves between devices by JAX's collectives and lax.ppermute only.
A program may use at most 128 MiB of HBM per device.

```python
import math
import jax
import jax.numpy as jnp
from jax import lax

K = 128
BS = 256
KB = 8
ITERS = 2
BRD = 8
NBR = 256
NODES = 65536
BC = 32
N_ROW = 8


def draw_blocks(key, part):
    key = jax.random.fold_in(key, 11)
    key_values, key_rows, key_cols = jax.random.split(key, 3)
    shape_full = (NBR, N_ROW, KB, BS, BS)
    row_scale = jnp.exp(jax.random.uniform(key_rows, (NBR, N_ROW, KB, BS, 1)) * math.log(10.0))
    col_scale = jnp.exp(jax.random.uniform(key_cols, (NBR, N_ROW, KB, 1, BS)) * math.log(10.0))
    source_panel = jnp.clip(jax.random.normal(key_values, shape_full), -4.0, 4.0)
    return (source_panel * row_scale * col_scale * 0.004).astype(jnp.bfloat16)


def draw_counts(key, part):
    key = jax.random.fold_in(key, 23)
    key_level, key_slots, key_place = jax.random.split(key, 3)
    col_total = NBR // BRD
    levels = jax.random.randint(key_level, (col_total, 1, N_ROW), 2, KB + 1)
    chosen = jax.random.randint(key_place, (), 0, col_total * N_ROW)
    places = jnp.arange(col_total * N_ROW).reshape(col_total, 1, N_ROW)
    levels = jnp.where(places == chosen, KB, levels)
    drawn = jax.random.randint(key_slots, (col_total, BRD, N_ROW), 0, 1 << 20)
    filled = drawn % levels + 1
    leading = jnp.arange(BRD).reshape(1, BRD, 1) == 0
    filled = jnp.where(leading, levels, filled)
    return filled.reshape(NBR, N_ROW).astype(jnp.int32)


def touch_ends(values, key, least, largest):
    longest = values.shape.index(max(values.shape))
    spots = []
    for shift in (0, 1):
        where = [jax.random.randint(jax.random.fold_in(key, axis), (), 0, length) for axis, length in enumerate(values.shape)]
        where[longest] = (where[longest] + shift) % values.shape[longest]
        spots.append(tuple(where))
    return values.at[spots[0]].set(least).at[spots[1]].set(largest)


def level_of(rng, extent, cuts, smallest, largest):
    def one(dim, shards_of):
        steps = jax.random.uniform(jax.random.fold_in(jax.random.fold_in(rng, 6), dim), (shards_of,), jnp.float32, smallest / len(cuts), largest / len(cuts))
        return jnp.repeat(jnp.exp(steps), extent[dim] // shards_of).reshape((-1,) + (1,) * (len(extent) - dim - 1))

    gain = one(*cuts[0])
    for cut in cuts[1:]:
        gain = gain * one(*cut)
    return gain


def noise(key, extent, deviation, most, shards=(), held_as=jnp.bfloat16):
    values = jax.random.normal(key, extent, jnp.float32) * deviation
    if len(shards) > 0:
        values = level_of(key, extent, shards, -0.22, 0.18) * values
    return jnp.clip(values, min=-most, max=most).astype(held_as)


def setup_inputs(seed: int = 0) -> dict:
    splits = jax.random.split(jax.random.key(seed), 5)
    return {
        "blocks": draw_blocks(jax.random.fold_in(splits[4], 71), 0),
        "block_cols": touch_ends(jax.random.randint(splits[1], (NBR, N_ROW, KB), 0, BC), jax.random.fold_in(splits[1], 1), 0, BC - 1).astype(jnp.int32),
        "counts": draw_counts(jax.random.fold_in(splits[4], 71), 0),
        "random_start_panel": noise(splits[3], (NODES, K), 1.0, 6.0, ((0, 256),)),
    }


def orthogonal(values):
    gram_matrix = jnp.dot(values.T, values, precision=lax.Precision.HIGHEST)
    factor = jnp.linalg.cholesky(gram_matrix)
    return jax.scipy.linalg.solve_triangular(factor, values.T, lower=True).T

def reference(blocks, block_cols, counts, random_start_panel):
    row_count = blocks.shape[1]
    depth = blocks.shape[2]
    width = blocks.shape[3]
    feature = random_start_panel.shape[1]
    rows_per_block = blocks.shape[0]
    alive = jnp.arange(depth)[None, None, :] < counts[:, :, None]
    neighbor_selector = ((block_cols[..., None] == jnp.arange(BC)[None, None, None, :]) & alive[..., None]).astype(jnp.float32)
    highest_precision = lax.Precision.HIGHEST

    def forward(vectors):
        grid_view = vectors.reshape(row_count, BC, width, feature)

        def one_row(pieces):
            tile_set, col_set, alive_set = pieces
            picked = grid_view[jnp.arange(row_count)[:, None], col_set].astype(jnp.float32)
            picked = picked * alive_set[..., None, None].astype(jnp.float32)
            return jnp.einsum('rkab,rkbn->an', tile_set.astype(jnp.float32), picked, precision=highest_precision)
        return lax.map(one_row, (blocks, block_cols, alive)).reshape(NODES, feature)

    def backward(vectors):
        rows_view = vectors.reshape(rows_per_block, width, feature)

        def add_row(total, pieces):
            tile_set, select_set, row_block = pieces
            block_products = jnp.einsum('rkab,an->rkbn', tile_set.astype(jnp.float32), row_block.astype(jnp.float32), precision=highest_precision)
            return (total + jnp.einsum('rkc,rkbn->rcbn', select_set, block_products, precision=highest_precision), None)
        total = jnp.zeros((row_count, BC, width, feature), jnp.float32)
        total, unused = lax.scan(add_row, total, (blocks, neighbor_selector, rows_view))
        return total.reshape(NODES, feature)
    current = random_start_panel
    result = None
    for sweep in range(ITERS):
        image = forward(current).astype(jnp.bfloat16)
        result = backward(image)
        if sweep + 1 < ITERS:
            current = result.astype(jnp.bfloat16)
    return orthogonal(result) * math.sqrt(NODES)
```

```python
import functools
import math

import jax
import jax.numpy as jnp
from jax import lax
from jax.experimental import pallas as pl
from jax.experimental.pallas import tpu as pltpu
from jax.sharding import PartitionSpec as P

ITERS = 2
CORE, ZLO, X = 1, 2, 8
Y, ZHI = 1, 4
DEAD = 32
TAIL = 16
STEPS = 32000.0
LEAST = 1e-30
VMEM = 57 << 20
BF, F32 = jnp.bfloat16, jnp.float32


def swap(value, axis, bits):
    size = lax.axis_size(axis)
    return lax.ppermute(value, axis, [(i, i ^ bits) for i in range(size)])


def encode(parts, ref):
    top = functools.reduce(jnp.maximum, [jnp.abs(part) for part in parts])
    top = jnp.maximum(jnp.max(top, axis=(0, 1), keepdims=True), LEAST)
    power = jnp.ceil(jnp.log2(top))
    scale = jnp.exp2(-power)
    high = parts[0].shape[0]
    for n, part in enumerate(parts):
        root = part * scale
        root = root * lax.rsqrt(jnp.abs(root) + LEAST)
        root = root * lax.rsqrt(jnp.abs(root) + LEAST)
        ref[n * high : (n + 1) * high] = jnp.round(root * STEPS).astype(jnp.int32).astype(jnp.int16)
    tail = jnp.broadcast_to(power, (TAIL, ref.shape[1]))
    ref[len(parts) * high :] = tail.astype(jnp.int32).astype(jnp.int16)


def decode(ref, high=128):
    count = (ref.shape[0] - TAIL) // high
    gain = jnp.exp2(ref[count * high :].astype(jnp.int32).astype(F32))[:1]
    parts = []
    for n in range(count):
        root = ref[n * high : (n + 1) * high].astype(jnp.int32).astype(F32) * (1.0 / STEPS)
        root = root * jnp.abs(root)
        parts.append(root * jnp.abs(root) * gain)
    return parts


def coded(count, feature=128, width=256):
    return jax.ShapeDtypeStruct((count * feature + TAIL, width), jnp.int16)


def plain(count, dtype=F32, feature=128, width=256):
    return jax.ShapeDtypeStruct((count, feature, width), dtype)


def local(kernel, outs, *args, slices=()):
    cut = [
        pl.BlockSpec((rows, *array.shape[1:]), lambda i, at=at: (at, 0, 0)) for array, rows, at in slices
    ]
    whole = lambda a: pl.BlockSpec(a.shape, lambda i, n=len(a.shape): (0,) * n)
    operands = [array for array, _, _ in slices] + list(args)
    return pl.pallas_call(
        kernel,
        grid=(1,),
        in_specs=cut + [whole(a) for a in args],
        out_specs=[whole(o) for o in outs],
        out_shape=outs,
        compiler_params=pltpu.CompilerParams(vmem_limit_bytes=24 << 20),
        cost_estimate=pl.CostEstimate(flops=1 << 20, bytes_accessed=2 << 20, transcendentals=0),
        name=kernel.__name__,
    )(*operands)


def far_x(keep, other, low, high):
    encode([keep[n] + other[n] for n in (0, 1)], low)
    encode([keep[n] + other[n] for n in (2, 3)], high)


def near_x(keep_first, keep_third, other, low, high, first, third):
    low, high = decode(low), decode(high)
    one = [keep_first[n] + other[n] for n in range(4)]
    encode([one[0] + low[0], one[1] + low[1], one[2], one[3]], first)
    three = [keep_third[n] + other[4 + n] for n in range(4)]
    encode([three[0], three[1], three[2] + high[0], three[3] + high[1]], third)


def own_x(keep, other, first, third, line, *far):
    first, third = decode(first), decode(third)
    total = [keep[n] + other[n] + (first[n] + third[n]) for n in range(4)]
    line[0] = total[0]
    for n in (1, 2, 3):
        encode([total[n]], far[n - 1])


def own_line(line, one, two, three, result, piece):
    total = line[0] + (decode(one)[0] + decode(two)[0] + decode(three)[0])
    result[0] = total
    piece[0] = total.astype(BF)


def own_y(near, one, two, three, total, far):
    parts = [decode(ref) for ref in (one, two, three)]
    sums = [near[n] + (parts[0][n] + parts[1][n] + parts[2][n]) for n in (0, 1)]
    total[0], total[1] = sums
    encode(sums, far)


def own_row(total, far, image):
    far = decode(far)
    for n in (0, 1):
        image[n] = (total[n] + far[n]).astype(BF)


def gather_col(piece):
    near = jnp.concatenate([piece] + [swap(piece, "col", ZLO * d) for d in (1, 2, 3)])
    first, third = swap(near, "col", X * 1), swap(near, "col", X * 3)
    low, high = swap(first[:2], "col", X * 3), swap(third[2:], "col", X * 1)
    parts = [near, first, low, high, third]
    return parts + [swap(part, "col", CORE) for part in parts]


def scatter_col(keep, send2, send13, send0):
    two, rest, zero = (swap(part, "col", CORE) for part in (send2, send13, send0))
    low, high = local(far_x, [coded(2)] * 2, two, slices=[(keep, 4, 2)])
    low, high = swap(low, "col", X * 3), swap(high, "col", X * 1)
    first, third = local(near_x, [coded(4)] * 2, rest, low, high, slices=[(keep, 4, 1), (keep, 4, 3)])
    first, third = swap(first, "col", X * 1), swap(third, "col", X * 3)
    line, *far = local(own_x, [plain(1)] + [coded(1)] * 3, zero, first, third, slices=[(keep, 4, 0)])
    far = [swap(far[d - 1], "col", ZLO * d) for d in (1, 2, 3)]
    return local(own_line, [plain(1), plain(1, BF)], line, *far)


def reduce_row(near, *far):
    far = [swap(far[d - 1], "row", Y * d) for d in (1, 2, 3)]
    total, code = local(own_y, [plain(2), coded(2)], near, *far)
    (share,) = local(own_row, [plain(2, BF)], total, swap(code, "row", ZHI))
    return [share] + [swap(share, "row", Y * d) for d in (1, 2, 3)]


def forward_kernel(slots, order, tiles, *refs):
    parts, (near, far1, far2, far3, panel, total) = refs[:10], refs[10:]
    step = pl.program_id(0)

    @pl.when(step == 0)
    def _():
        at = 0
        for part in parts:
            panel[at : at + part.shape[0]] = part[...]
            at += part.shape[0]
        panel[DEAD] = jnp.zeros(panel.shape[1:], panel.dtype)

    rows = None
    for k in range(tiles.shape[1]):
        part = lax.dot_general(
            panel[slots[step, k]], tiles[0, k], (((1,), (1,)), ((), ())), preferred_element_type=F32
        )
        rows = part if rows is None else rows + part
    total[step] = rows

    @pl.when(step == pl.num_programs(0) - 1)
    def _():
        near[...] = total[0:2]
        for d, far in enumerate((far1, far2, far3)):
            encode([total[2 * d + 2], total[2 * d + 3]], far)


def sweep_spec(tiles, operands, outs, scratch):
    rows, depth, width, _ = tiles.shape
    whole = lambda a: pl.BlockSpec(a.shape, lambda i, s, o, n=len(a.shape): (0,) * n)
    return pltpu.PrefetchScalarGridSpec(
        num_scalar_prefetch=2,
        grid=(rows,),
        in_specs=[pl.BlockSpec((1, depth, width, width), lambda i, s, o: (o[i], 0, 0, 0))]
        + [whole(a) for a in operands],
        out_specs=[whole(o) for o in outs],
        scratch_shapes=scratch,
    )


def sweep_call(kernel, slots, order, tiles, operands, outs, scratch):
    return pl.pallas_call(
        kernel,
        grid_spec=sweep_spec(tiles, operands, outs, scratch),
        out_shape=outs,
        compiler_params=pltpu.CompilerParams(vmem_limit_bytes=VMEM),
        cost_estimate=pl.CostEstimate(flops=2 * 64 * 256 * 256 * 128, bytes_accessed=12 << 20, transcendentals=0),
        name=kernel.__name__,
    )(slots, order, tiles, *operands)


def forward(slots, order, tiles, parts):
    outs = [plain(2)] + [coded(2)] * 3
    scratch = [pltpu.VMEM((DEAD + 1, 128, 256), BF), pltpu.VMEM((8, 128, 256), F32)]
    return sweep_call(forward_kernel, slots, order, tiles, parts, outs, scratch)


def backward_kernel(slots, order, tiles, a, b, c, d, keep, send2, send13, send0, image, total):
    step = pl.program_id(0)

    @pl.when(step == 0)
    def _():
        for q, ref in enumerate((a, b, c, d)):
            image[2 * q : 2 * q + 2] = ref[...]
        total[...] = jnp.zeros(total.shape, total.dtype)

    rows = image[step]
    for k in range(tiles.shape[1]):
        total[slots[step, k]] += jnp.dot(rows, tiles[0, k], preferred_element_type=F32)

    @pl.when(step == pl.num_programs(0) - 1)
    def _():
        keep[...] = total[0:16]
        send0[...] = total[16:20]
        send13[0:4] = total[20:24]
        send2[...] = total[24:28]
        send13[4:8] = total[28:32]


def backward(slots, order, tiles, parts):
    outs = [plain(16), plain(4), plain(8), plain(4)]
    scratch = [pltpu.VMEM((8, 128, 256), BF), pltpu.VMEM((DEAD + 1, 128, 256), F32)]
    return sweep_call(backward_kernel, slots, order, tiles, parts, outs, scratch)


def all_sum(value):
    value = value + swap(value, "col", CORE)
    value = value + sum(swap(value, "col", X * d) for d in (1, 2, 3))
    value = value + sum(swap(value, "col", ZLO * d) for d in (1, 2, 3))
    value = value + sum(swap(value, "row", Y * d) for d in (1, 2, 3))
    return value + swap(value, "row", ZHI)


def body(blocks, block_cols, counts, random_start_panel):
    col, row = lax.axis_index("col"), lax.axis_index("row")
    tiles = blocks[:, 0]
    order = jnp.arange(tiles.shape[0], dtype=jnp.int32) ^ (2 * (row % 4))
    away = block_cols[:, 0] ^ col
    away = (away % 2) * 16 + away // 2
    alive = jnp.arange(tiles.shape[1])[None, :] < counts[:, 0][:, None]
    slots = jnp.where(alive, away, DEAD)[order]
    piece = random_start_panel.T[None]
    result = None
    for _ in range(ITERS):
        image = reduce_row(*forward(slots, order, tiles, gather_col(piece)))
        result, piece = scatter_col(*backward(slots, order, tiles, image))
    result = result[0]
    gram = all_sum(jnp.dot(result, result.T, precision=lax.Precision.HIGHEST))
    factor = jnp.linalg.cholesky(gram)
    nodes = lax.axis_size("row") * lax.axis_size("col") * result.shape[1]
    return jax.scipy.linalg.solve_triangular(factor, result, lower=True).T * math.sqrt(nodes)


def solution(mesh):
    return jax.shard_map(
        body,
        mesh=mesh,
        in_specs=(
            P("col", "row", None, None, None),
            P("col", "row", None),
            P("col", "row"),
            P(("row", "col"), None),
        ),
        out_specs=P(("row", "col"), None),
        check_vma=False,
    )
```

```python
import functools
import math

import jax
import jax.numpy as jnp
from jax import lax
from jax.experimental import pallas as pl
from jax.experimental.pallas import tpu as pltpu
from jax.sharding import PartitionSpec as P

ITERS = 2
CORE, ZLO, X = 1, 2, 8
Y, ZHI = 1, 4
DEAD = 32
TAIL = 16
STEPS = 32000.0
LEAST = 1e-30
VMEM = 24 << 20
BF, F32 = jnp.bfloat16, jnp.float32
HIGHEST = lax.Precision.HIGHEST


def swap(value, axis, bits):
    size = lax.axis_size(axis)
    return lax.ppermute(value, axis, [(i, i ^ bits) for i in range(size)])


def encode(parts, ref):
    top = functools.reduce(jnp.maximum, [jnp.abs(part) for part in parts])
    top = jnp.maximum(jnp.max(top, axis=(0, 1), keepdims=True), LEAST)
    power = jnp.ceil(jnp.log2(top))
    scale = jnp.exp2(-power)
    high = parts[0].shape[0]
    for n, part in enumerate(parts):
        root = part * scale
        root = root * lax.rsqrt(jnp.abs(root) + LEAST)
        root = root * lax.rsqrt(jnp.abs(root) + LEAST)
        ref[n * high : (n + 1) * high] = jnp.round(root * STEPS).astype(jnp.int32).astype(jnp.int16)
    tail = jnp.broadcast_to(power, (TAIL, ref.shape[1]))
    ref[len(parts) * high :] = tail.astype(jnp.int32).astype(jnp.int16)


def decode(ref, high=128):
    count = (ref.shape[0] - TAIL) // high
    gain = jnp.exp2(ref[count * high :].astype(jnp.int32).astype(F32))[:1]
    parts = []
    for n in range(count):
        root = ref[n * high : (n + 1) * high].astype(jnp.int32).astype(F32) * (1.0 / STEPS)
        root = root * jnp.abs(root)
        parts.append(root * jnp.abs(root) * gain)
    return parts


def coded(count, feature=128, width=256):
    return jax.ShapeDtypeStruct((count * feature + TAIL, width), jnp.int16)


def plain(count, dtype=F32, feature=128, width=256):
    return jax.ShapeDtypeStruct((count, feature, width), dtype)


def local(kernel, outs, *args, slices=()):
    cut = [
        pl.BlockSpec((rows, *array.shape[1:]), lambda i, at=at: (at, 0, 0)) for array, rows, at in slices
    ]
    whole = lambda a: pl.BlockSpec(a.shape, lambda i, n=len(a.shape): (0,) * n)
    operands = [array for array, _, _ in slices] + list(args)
    return pl.pallas_call(
        kernel,
        grid=(1,),
        in_specs=cut + [whole(a) for a in args],
        out_specs=[whole(o) for o in outs],
        out_shape=outs,
        compiler_params=pltpu.CompilerParams(vmem_limit_bytes=24 << 20),
        cost_estimate=pl.CostEstimate(flops=1 << 20, bytes_accessed=2 << 20, transcendentals=0),
        name=kernel.__name__,
    )(*operands)


def far_x(keep, other, low, high):
    encode([keep[n] + other[n] for n in (0, 1)], low)
    encode([keep[n] + other[n] for n in (2, 3)], high)


def near_x(keep_first, keep_third, other, low, high, first, third):
    low, high = decode(low), decode(high)
    one = [keep_first[n] + other[n] for n in range(4)]
    encode([one[0] + low[0], one[1] + low[1], one[2], one[3]], first)
    three = [keep_third[n] + other[4 + n] for n in range(4)]
    encode([three[0], three[1], three[2] + high[0], three[3] + high[1]], third)


def own_x(keep, other, first, third, line, *far):
    first, third = decode(first), decode(third)
    total = [keep[n] + other[n] + (first[n] + third[n]) for n in range(4)]
    line[0] = total[0]
    for n in (1, 2, 3):
        encode([total[n]], far[n - 1])


def own_line(line, one, two, three, result, piece):
    total = line[0] + (decode(one)[0] + decode(two)[0] + decode(three)[0])
    result[0] = total
    piece[0] = total.astype(BF)


def own_y(near, one, two, three, total, far):
    parts = [decode(ref) for ref in (one, two, three)]
    sums = [near[n] + (parts[0][n] + parts[1][n] + parts[2][n]) for n in (0, 1)]
    total[0], total[1] = sums
    encode(sums, far)


def own_row(total, far, image):
    far = decode(far)
    for n in (0, 1):
        image[n] = (total[n] + far[n]).astype(BF)


def gather_col(piece):
    near = jnp.concatenate([piece] + [swap(piece, "col", ZLO * d) for d in (1, 2, 3)])
    first, third = swap(near, "col", X * 1), swap(near, "col", X * 3)
    low, high = swap(first[:2], "col", X * 3), swap(third[2:], "col", X * 1)
    parts = [near, first, low, high, third]
    return parts + [swap(part, "col", CORE) for part in parts]


def scatter_col(keep, send2, send13, send0):
    two, rest, zero = (swap(part, "col", CORE) for part in (send2, send13, send0))
    low, high = local(far_x, [coded(2)] * 2, two, slices=[(keep, 4, 2)])
    low, high = swap(low, "col", X * 3), swap(high, "col", X * 1)
    first, third = local(near_x, [coded(4)] * 2, rest, low, high, slices=[(keep, 4, 1), (keep, 4, 3)])
    first, third = swap(first, "col", X * 1), swap(third, "col", X * 3)
    line, *far = local(own_x, [plain(1)] + [coded(1)] * 3, zero, first, third, slices=[(keep, 4, 0)])
    far = [swap(far[d - 1], "col", ZLO * d) for d in (1, 2, 3)]
    return local(own_line, [plain(1), plain(1, BF)], line, *far)


def reduce_row(near, *far):
    far = [swap(far[d - 1], "row", Y * d) for d in (1, 2, 3)]
    total, code = local(own_y, [plain(2), coded(2)], near, *far)
    (share,) = local(own_row, [plain(2, BF)], total, swap(code, "row", ZHI))
    return [share] + [swap(share, "row", Y * d) for d in (1, 2, 3)]


def slot_of(cols, counts, i, k):
    away = cols[i, 0, k] ^ lax.axis_index("col")
    return jnp.where(k < counts[i, 0], (away % 2) * 16 + away // 2, DEAD)


def block_row(step):
    return step ^ (2 * (lax.axis_index("row") % 4))


def forward_kernel(cols, counts, tiles, *refs):
    parts, (near, far1, far2, far3, panel) = refs[:10], refs[10:]
    at = 0
    for part in parts:
        panel[at : at + part.shape[0]] = part[...]
        at += part.shape[0]
    panel[DEAD] = jnp.zeros(panel.shape[1:], panel.dtype)

    def rows(step):
        i, total = block_row(step), None
        for k in range(tiles.shape[1]):
            part = lax.dot_general(
                panel[slot_of(cols, counts, i, k)],
                tiles[i, k],
                (((1,), (1,)), ((), ())),
                preferred_element_type=F32,
            )
            total = part if total is None else total + part
        return total

    for d, far in enumerate((far1, far2, far3)):
        encode([rows(2 * d + 2), rows(2 * d + 3)], far)
    near[0], near[1] = rows(0), rows(1)


def sweep_call(kernel, cols, counts, tiles, operands, outs, scratch):
    vmem, smem = pl.BlockSpec(memory_space=pltpu.VMEM), pl.BlockSpec(memory_space=pltpu.SMEM)
    return pl.pallas_call(
        kernel,
        in_specs=[smem, smem] + [vmem] * (1 + len(operands)),
        out_specs=[vmem] * len(outs),
        out_shape=outs,
        scratch_shapes=scratch,
        compiler_params=pltpu.CompilerParams(vmem_limit_bytes=VMEM),
        cost_estimate=pl.CostEstimate(flops=2 * 64 * 256 * 256 * 128, bytes_accessed=4 << 20, transcendentals=0),
        name=kernel.__name__,
    )(cols, counts, tiles, *operands)


def forward(cols, counts, tiles, parts):
    outs = [plain(2)] + [coded(2)] * 3
    return sweep_call(forward_kernel, cols, counts, tiles, parts, outs, [pltpu.VMEM((DEAD + 1, 128, 256), BF)])


def backward_kernel(cols, counts, tiles, a, b, c, d, keep, send2, send13, send0, total):
    total[...] = jnp.zeros(total.shape, total.dtype)
    for q, ref in enumerate((a, b, c, d)):
        for half in (0, 1):
            i = block_row(2 * q + half)
            for k in range(tiles.shape[1]):
                total[slot_of(cols, counts, i, k)] += jnp.dot(ref[half], tiles[i, k], preferred_element_type=F32)
    keep[...] = total[0:16]
    send0[...] = total[16:20]
    send13[0:4] = total[20:24]
    send2[...] = total[24:28]
    send13[4:8] = total[28:32]


def backward(cols, counts, tiles, parts):
    outs = [plain(16), plain(4), plain(8), plain(4)]
    return sweep_call(backward_kernel, cols, counts, tiles, parts, outs, [pltpu.VMEM((DEAD + 1, 128, 256), F32)])


def gram_kernel(result, gram):
    gram[...] = lax.dot_general(
        result[0], result[0], (((1,), (1,)), ((), ())), precision=HIGHEST, preferred_element_type=F32
    )


def split_gram(gram, other, near, one, two, three, total):
    total[...] = gram[...] + other[...]
    x = lax.axis_index("col") // X
    for d, ref in enumerate((near, one, two, three)):
        ref[...] = total[pl.ds(pl.multiple_of((x ^ d) * 32, 32), 32)]


def all_sum(gram):
    vmem = pl.BlockSpec(memory_space=pltpu.VMEM)
    parts = pl.pallas_call(
        split_gram,
        in_specs=[vmem] * 2,
        out_specs=[vmem] * 4,
        out_shape=[jax.ShapeDtypeStruct((32, 128), F32)] * 4,
        scratch_shapes=[pltpu.VMEM((128, 128), F32)],
        name="split_gram",
    )(gram, swap(gram, "col", CORE))

    def four(value, axis, bits):
        one, two, three = (swap(value, axis, bits * d) for d in (1, 2, 3))
        return (value + one) + (two + three)

    one, two, three = (swap(parts[d], "col", X * d) for d in (1, 2, 3))
    strip = four(four((parts[0] + one) + (two + three), "col", ZLO), "row", Y)
    strip = strip + swap(strip, "row", ZHI)
    return [strip] + [swap(strip, "col", X * d) for d in (1, 2, 3)]


def basis_kernel(near, one, two, three, result, out, gram, *, factor):
    n, step = gram.shape[0], 16
    x = lax.axis_index("col") // X
    for d, ref in enumerate((near, one, two, three)):
        gram[pl.ds(pl.multiple_of((x ^ d) * 32, 32), 32)] = ref[...]
    row = lax.broadcasted_iota(jnp.int32, (n, n), 0)
    lane = lax.broadcasted_iota(jnp.int32, (n, n), 1)
    left = jnp.concatenate([gram[...], jnp.where(row == lane, 1.0, 0.0)], axis=1)
    row, lane = row[:step], lane[:step]
    inverse = []
    for at in range(0, n, step):
        upper, lower = left[at : at + step, :n], left[at : at + step, n:]
        columns = [jnp.broadcast_to(upper[:, at + c : at + c + 1], (step, n)) for c in range(step)]
        pivots = jnp.zeros((step, n), F32)
        for j in range(step):
            pivot = 1.0 / columns[j][j : j + 1]
            ratio = jnp.where(row > j, columns[j] * pivot, 0.0)
            for c in range(j + 1, step):
                columns[c] = columns[c] - ratio * columns[c][j : j + 1]
            upper = upper - ratio * upper[j : j + 1]
            lower = lower - ratio * lower[j : j + 1]
            pivots = jnp.where(row == j, pivot, pivots)
        inverse.append(lower * (jnp.sqrt(pivots) * factor))
        if at + step < n:
            ratio = jnp.where(lane >= at + step, upper * pivots, 0.0)
            left = left - lax.dot_general(
                ratio,
                jnp.concatenate([upper, lower], axis=1),
                (((0,), (0,)), ((), ())),
                precision=HIGHEST,
                preferred_element_type=F32,
            )
    inverse = jnp.concatenate(inverse, axis=0)
    out[...] = jnp.dot(inverse, result[0], precision=HIGHEST, preferred_element_type=F32).T


def body(blocks, block_cols, counts, random_start_panel):
    tiles = blocks[:, 0]
    vmem = pl.BlockSpec(memory_space=pltpu.VMEM)
    piece = random_start_panel.T[None]
    result = None
    for _ in range(ITERS):
        image = reduce_row(*forward(block_cols, counts, tiles, gather_col(piece)))
        result, piece = scatter_col(*backward(block_cols, counts, tiles, image))
    feature, width = result.shape[1:]
    gram = pl.pallas_call(
        gram_kernel,
        in_specs=[vmem],
        out_specs=vmem,
        out_shape=jax.ShapeDtypeStruct((feature, feature), F32),
        name="gram",
    )(result)
    nodes = lax.axis_size("row") * lax.axis_size("col") * width
    return pl.pallas_call(
        functools.partial(basis_kernel, factor=math.sqrt(nodes)),
        in_specs=[vmem] * 5,
        out_specs=vmem,
        out_shape=jax.ShapeDtypeStruct((width, feature), F32),
        scratch_shapes=[pltpu.VMEM((feature, feature), F32)],
        compiler_params=pltpu.CompilerParams(vmem_limit_bytes=VMEM),
        name="basis",
    )(*all_sum(gram), result)


def solution(mesh):
    return jax.shard_map(
        body,
        mesh=mesh,
        in_specs=(
            P("col", "row", None, None, None),
            P("col", "row", None),
            P("col", "row"),
            P(("row", "col"), None),
        ),
        out_specs=P(("row", "col"), None),
        check_vma=False,
    )
```

```python
import functools
import math

import jax
import jax.numpy as jnp
from jax import lax
from jax.experimental import pallas as pl
from jax.experimental.pallas import tpu as pltpu
from jax.sharding import PartitionSpec as P

ITERS = 2
CORE, ZLO, X = 1, 2, 8
Y, ZHI = 1, 4
DEAD = 32
TAIL = 16
STEPS = 32000.0
LEAST = 1e-30
VMEM = 24 << 20
BF, F32 = jnp.bfloat16, jnp.float32
HIGHEST = lax.Precision.HIGHEST


def swap(value, axis, bits):
    size = lax.axis_size(axis)
    return lax.ppermute(value, axis, [(i, i ^ bits) for i in range(size)])


def encode(parts, ref):
    top = functools.reduce(jnp.maximum, [jnp.abs(part) for part in parts])
    top = jnp.maximum(jnp.max(top, axis=(0, 1), keepdims=True), LEAST)
    power = jnp.ceil(jnp.log2(top))
    scale = jnp.exp2(-power)
    high = parts[0].shape[0]
    for n, part in enumerate(parts):
        root = part * scale
        root = root * lax.rsqrt(jnp.abs(root) + LEAST)
        root = root * lax.rsqrt(jnp.abs(root) + LEAST)
        ref[n * high : (n + 1) * high] = jnp.round(root * STEPS).astype(jnp.int32).astype(jnp.int16)
    tail = jnp.broadcast_to(power, (TAIL, ref.shape[1]))
    ref[len(parts) * high :] = tail.astype(jnp.int32).astype(jnp.int16)


def decode(ref, high=128):
    count = (ref.shape[0] - TAIL) // high
    gain = jnp.exp2(ref[count * high :].astype(jnp.int32).astype(F32))[:1]
    parts = []
    for n in range(count):
        root = ref[n * high : (n + 1) * high].astype(jnp.int32).astype(F32) * (1.0 / STEPS)
        root = root * jnp.abs(root)
        parts.append(root * jnp.abs(root) * gain)
    return parts


def coded(count, feature=128, width=256):
    return jax.ShapeDtypeStruct((count * feature + TAIL, width), jnp.int16)


def plain(count, dtype=F32, feature=128, width=256):
    return jax.ShapeDtypeStruct((count, feature, width), dtype)


def local(kernel, outs, *args, scratch=(), limit=8):
    vmem = pl.BlockSpec(memory_space=pltpu.VMEM)
    return pl.pallas_call(
        kernel,
        in_specs=[vmem] * len(args),
        out_specs=[vmem] * len(outs),
        out_shape=outs,
        scratch_shapes=scratch,
        compiler_params=pltpu.CompilerParams(vmem_limit_bytes=limit << 20),
        cost_estimate=pl.CostEstimate(flops=1 << 20, bytes_accessed=1 << 20, transcendentals=0),
        name=kernel.__name__,
    )(*args)


def far_x(keep, other, low, high):
    encode([keep[8 + n] + other[n] for n in (0, 1)], low)
    encode([keep[8 + n] + other[n] for n in (2, 3)], high)


def near_x(keep, other, low, high, first, third):
    low, high = decode(low), decode(high)
    one = [keep[4 + n] + other[n] for n in range(4)]
    encode([one[0] + low[0], one[1] + low[1], one[2], one[3]], first)
    three = [keep[12 + n] + other[4 + n] for n in range(4)]
    encode([three[0], three[1], three[2] + high[0], three[3] + high[1]], third)


def own_x(keep, other, first, third, line, *far):
    first, third = decode(first), decode(third)
    total = [keep[n] + other[n] + (first[n] + third[n]) for n in range(4)]
    line[0] = total[0]
    for n in (1, 2, 3):
        encode([total[n]], far[n - 1])


def own_line(line, one, two, three, piece):
    piece[0] = (line[0] + (decode(one)[0] + decode(two)[0] + decode(three)[0])).astype(BF)


def last_line(line, one, two, three, result, gram):
    total = line[0] + (decode(one)[0] + decode(two)[0] + decode(three)[0])
    result[0] = total
    gram[...] = lax.dot_general(
        total, total, (((1,), (1,)), ((), ())), precision=HIGHEST, preferred_element_type=F32
    )


def own_y(near, one, two, three, total, far):
    parts = [decode(ref) for ref in (one, two, three)]
    sums = [near[n] + (parts[0][n] + parts[1][n] + parts[2][n]) for n in (0, 1)]
    total[0], total[1] = sums
    encode(sums, far)


def own_row(total, far, image):
    far = decode(far)
    for n in (0, 1):
        image[n] = (total[n] + far[n]).astype(BF)


def join(a, b, c, d, *refs):
    for n, ref in enumerate((a, b, c, d)):
        refs[-1][n] = ref[0]


def gather_col(piece, *after):
    line = [piece] + [swap(piece, "col", ZLO * d) for d in (1, 2, 3)]
    (near,) = local(join, [plain(4, BF)], *line, *after)
    first, third = swap(near, "col", X * 1), swap(near, "col", X * 3)
    low, high = swap(first[:2], "col", X * 3), swap(third[2:], "col", X * 1)
    parts = [near, first, low, high, third]
    return parts + [swap(part, "col", CORE) for part in parts]


def scatter_col(keep, send2, send13, send0):
    two, rest, zero = (swap(part, "col", CORE) for part in (send2, send13, send0))
    low, high = local(far_x, [coded(2)] * 2, keep, two)
    low, high = swap(low, "col", X * 3), swap(high, "col", X * 1)
    first, third = local(near_x, [coded(4)] * 2, keep, rest, low, high)
    first, third = swap(first, "col", X * 1), swap(third, "col", X * 3)
    line, *far = local(own_x, [plain(1)] + [coded(1)] * 3, keep, zero, first, third)
    return [line] + [swap(far[d - 1], "col", ZLO * d) for d in (1, 2, 3)]


def reduce_row(near, *far):
    far = [swap(far[d - 1], "row", Y * d) for d in (1, 2, 3)]
    total, code = local(own_y, [plain(2), coded(2)], near, *far)
    (share,) = local(own_row, [plain(2, BF)], total, swap(code, "row", ZHI))
    return [share] + [swap(share, "row", Y * d) for d in (1, 2, 3)]


def slot_of(cols, counts, i, k):
    away = cols[i, 0, k] ^ lax.axis_index("col")
    return jnp.where(k < counts[i], (away % 2) * 16 + away // 2, DEAD)


def block_row(step):
    return step ^ (2 * (lax.axis_index("row") % 4))


def forward_kernel(cols, counts, tiles, *refs):
    parts, (near, far1, far2, far3, panel) = refs[:10], refs[10:]
    at = 0
    for part in parts:
        panel[at : at + part.shape[0]] = part[...]
        at += part.shape[0]
    panel[DEAD] = jnp.zeros(panel.shape[1:], panel.dtype)

    def rows(step):
        i, total = block_row(step), None
        for k in range(tiles.shape[1]):
            part = lax.dot_general(
                panel[slot_of(cols, counts, i, k)],
                tiles[i, k],
                (((1,), (1,)), ((), ())),
                preferred_element_type=F32,
            )
            total = part if total is None else total + part
        return total

    for d, far in enumerate((far1, far2, far3)):
        encode([rows(2 * d + 2), rows(2 * d + 3)], far)
    near[0], near[1] = rows(0), rows(1)


def sweep_call(kernel, cols, counts, tiles, operands, outs, scratch):
    vmem, smem = pl.BlockSpec(memory_space=pltpu.VMEM), pl.BlockSpec(memory_space=pltpu.SMEM)
    return pl.pallas_call(
        kernel,
        in_specs=[smem, smem] + [vmem] * (1 + len(operands)),
        out_specs=[vmem] * len(outs),
        out_shape=outs,
        scratch_shapes=scratch,
        compiler_params=pltpu.CompilerParams(vmem_limit_bytes=VMEM),
        cost_estimate=pl.CostEstimate(flops=2 * 64 * 256 * 256 * 128, bytes_accessed=4 << 20, transcendentals=0),
        name=kernel.__name__,
    )(cols, counts, tiles, *operands)


def forward(cols, counts, tiles, parts):
    outs = [plain(2)] + [coded(2)] * 3
    return sweep_call(forward_kernel, cols, counts, tiles, parts, outs, [pltpu.VMEM((DEAD + 1, 128, 256), BF)])


def backward_kernel(cols, counts, tiles, a, b, c, d, keep, send2, send13, send0, total):
    total[...] = jnp.zeros(total.shape, total.dtype)
    for q, ref in enumerate((a, b, c, d)):
        for half in (0, 1):
            i = block_row(2 * q + half)
            for k in range(tiles.shape[1]):
                total[slot_of(cols, counts, i, k)] += jnp.dot(ref[half], tiles[i, k], preferred_element_type=F32)
    keep[...] = total[0:16]
    send0[...] = total[16:20]
    send13[0:4] = total[20:24]
    send2[...] = total[24:28]
    send13[4:8] = total[28:32]


def backward(cols, counts, tiles, parts):
    outs = [plain(16), plain(4), plain(8), plain(4)]
    return sweep_call(backward_kernel, cols, counts, tiles, parts, outs, [pltpu.VMEM((DEAD + 1, 128, 256), F32)])


def odd_swap(value, axes, bits):
    col, row = lax.axis_size("col"), lax.axis_size("row")
    pairs = [(r * col + c, (r ^ bits[0]) * col + (c ^ bits[1])) for r in range(row) for c in range(1, col, 2)]
    return lax.ppermute(value, axes, pairs)


def all_sum(gram):
    axes = ("row", "col")
    total = gram + swap(gram, "col", CORE)
    for bits in ((0, X), (0, ZLO), (Y, 0)):
        one, two, three = (odd_swap(total, axes, (bits[0] * d, bits[1] * d)) for d in (1, 2, 3))
        total = (total + one) + (two + three)
    total = total + odd_swap(total, axes, (ZHI, 0))
    return total, swap(total, "col", CORE)


def basis_kernel(own, other, result, out, *, factor):
    n, step = own.shape[0], 16
    gram = jnp.where(lax.axis_index("col") % 2 == 1, own[...], other[...])
    row = lax.broadcasted_iota(jnp.int32, (n, n), 0)
    lane = lax.broadcasted_iota(jnp.int32, (n, n), 1)
    left = jnp.concatenate([gram, jnp.where(row == lane, 1.0, 0.0)], axis=1)
    row, lane = row[:step], lane[:step]
    inverse = []
    for at in range(0, n, step):
        upper, lower = left[at : at + step, :n], left[at : at + step, n:]
        columns = [jnp.broadcast_to(upper[:, at + c : at + c + 1], (step, n)) for c in range(step)]
        pivots = jnp.zeros((step, n), F32)
        for j in range(step):
            pivot = 1.0 / columns[j][j : j + 1]
            ratio = jnp.where(row > j, columns[j] * pivot, 0.0)
            for c in range(j + 1, step):
                columns[c] = columns[c] - ratio * columns[c][j : j + 1]
            upper = upper - ratio * upper[j : j + 1]
            lower = lower - ratio * lower[j : j + 1]
            pivots = jnp.where(row == j, pivot, pivots)
        inverse.append(lower * (jnp.sqrt(pivots) * factor))
        if at + step < n:
            ratio = jnp.where(lane >= at + step, upper * pivots, 0.0)
            left = left - lax.dot_general(
                ratio,
                jnp.concatenate([upper, lower], axis=1),
                (((0,), (0,)), ((), ())),
                precision=HIGHEST,
                preferred_element_type=F32,
            )
    inverse = jnp.concatenate(inverse, axis=0)
    out[...] = jnp.dot(inverse, result[0], precision=HIGHEST, preferred_element_type=F32).T


def touch(blocks, token):
    token[...] = jnp.zeros(token.shape, token.dtype)


def body(blocks, block_cols, counts, random_start_panel):
    counts = counts.reshape(-1)
    tiles = blocks[:, 0]
    (token,) = local(touch, [jax.ShapeDtypeStruct((8, 128), F32)], tiles)
    parts = gather_col(random_start_panel.T[None], token)
    for sweep in range(ITERS):
        image = reduce_row(*forward(block_cols, counts, tiles, parts))
        line = scatter_col(*backward(block_cols, counts, tiles, image))
        if sweep + 1 < ITERS:
            (piece,) = local(own_line, [plain(1, BF)], *line)
            parts = gather_col(piece)
    feature, width = line[0].shape[1:]
    result, gram = local(last_line, [plain(1), jax.ShapeDtypeStruct((feature, feature), F32)], *line)
    nodes = lax.axis_size("row") * lax.axis_size("col") * width

    def basis(*refs):
        basis_kernel(*refs, factor=math.sqrt(nodes))

    return local(basis, [jax.ShapeDtypeStruct((width, feature), F32)], *all_sum(gram), result)[0]


def solution(mesh):
    return jax.shard_map(
        body,
        mesh=mesh,
        in_specs=(
            P("col", "row", None, None, None),
            P("col", "row", None),
            P("col", "row"),
            P(("row", "col"), None),
        ),
        out_specs=P(("row", "col"), None),
        check_vma=False,
    )
```

```python
import functools
import math

import jax
import jax.numpy as jnp
from jax import lax
from jax.experimental import pallas as pl
from jax.experimental.pallas import tpu as pltpu
from jax.sharding import PartitionSpec as P

ITERS = 2
CORE, ZLO, X = 1, 2, 8
Y, ZHI = 1, 4
DEAD = 32
TAIL = 16
STEPS = 32000.0
LEAST = 1e-30
BF, F32 = jnp.bfloat16, jnp.float32
HIGHEST = lax.Precision.HIGHEST


def swap(value, axis, bits):
    size = lax.axis_size(axis)
    return lax.ppermute(value, axis, [(i, i ^ bits) for i in range(size)])


def encode(parts, ref):
    top = functools.reduce(jnp.maximum, [jnp.abs(part) for part in parts])
    top = jnp.maximum(jnp.max(top, axis=(0, 1), keepdims=True), LEAST)
    power = jnp.ceil(jnp.log2(top))
    scale = jnp.exp2(-power)
    high = parts[0].shape[0]
    for n, part in enumerate(parts):
        root = part * scale
        root = root * lax.rsqrt(jnp.abs(root) + LEAST)
        root = root * lax.rsqrt(jnp.abs(root) + LEAST)
        ref[n * high : (n + 1) * high] = jnp.round(root * STEPS).astype(jnp.int32).astype(jnp.int16)
    tail = jnp.broadcast_to(power, (TAIL, ref.shape[1]))
    ref[len(parts) * high :] = tail.astype(jnp.int32).astype(jnp.int16)


def decode(ref, high=128):
    count = (ref.shape[0] - TAIL) // high
    gain = jnp.exp2(ref[count * high :].astype(jnp.int32).astype(F32))[:1]
    parts = []
    for n in range(count):
        root = ref[n * high : (n + 1) * high].astype(jnp.int32).astype(F32) * (1.0 / STEPS)
        root = root * jnp.abs(root)
        parts.append(root * jnp.abs(root) * gain)
    return parts


def coded(count, feature=128, width=256):
    return jax.ShapeDtypeStruct((count * feature + TAIL, width), jnp.int16)


def plain(count, dtype=F32, feature=128, width=256):
    return jax.ShapeDtypeStruct((count, feature, width), dtype)


def local(kernel, outs, *args, scratch=(), limit=8):
    vmem = pl.BlockSpec(memory_space=pltpu.VMEM)
    return pl.pallas_call(
        kernel,
        in_specs=[vmem] * len(args),
        out_specs=[vmem] * len(outs),
        out_shape=outs,
        scratch_shapes=scratch,
        compiler_params=pltpu.CompilerParams(vmem_limit_bytes=limit << 20),
        cost_estimate=pl.CostEstimate(flops=1 << 20, bytes_accessed=1 << 20, transcendentals=0),
        name=kernel.__name__,
    )(*args)


def far_x(keep, other, low, high):
    encode([keep[8 + n] + other[n] for n in (0, 1)], low)
    encode([keep[8 + n] + other[n] for n in (2, 3)], high)


def near_x(keep, other, low, high, first, third):
    low, high = decode(low), decode(high)
    one = [keep[4 + n] + other[n] for n in range(4)]
    encode([one[0] + low[0], one[1] + low[1], one[2], one[3]], first)
    three = [keep[12 + n] + other[4 + n] for n in range(4)]
    encode([three[0], three[1], three[2] + high[0], three[3] + high[1]], third)


def own_x(keep, other, first, third, line, *far):
    first, third = decode(first), decode(third)
    total = [keep[n] + other[n] + (first[n] + third[n]) for n in range(4)]
    line[0] = total[0]
    for n in (1, 2, 3):
        encode([total[n]], far[n - 1])


def own_line(line, one, two, three, piece):
    piece[0] = (line[0] + (decode(one)[0] + decode(two)[0] + decode(three)[0])).astype(BF)


def last_line(line, one, two, three, result, gram):
    total = line[0] + (decode(one)[0] + decode(two)[0] + decode(three)[0])
    result[0] = total
    gram[...] = lax.dot_general(
        total, total, (((1,), (1,)), ((), ())), precision=HIGHEST, preferred_element_type=F32
    )


def own_y(near, one, two, three, total, far):
    parts = [decode(ref) for ref in (one, two, three)]
    sums = [near[n] + (parts[0][n] + parts[1][n] + parts[2][n]) for n in (0, 1)]
    total[0], total[1] = sums
    encode(sums, far)


def own_row(total, far, image):
    far = decode(far)
    for n in (0, 1):
        image[n] = (total[n] + far[n]).astype(BF)


def join(a, b, c, d, *refs):
    for n, ref in enumerate((a, b, c, d)):
        refs[-1][n] = ref[0]


def gather_col(piece, *after):
    line = [piece] + [swap(piece, "col", ZLO * d) for d in (1, 2, 3)]
    (near,) = local(join, [plain(4, BF)], *line, *after)
    first, third = swap(near, "col", X * 1), swap(near, "col", X * 3)
    low, high = swap(first[:2], "col", X * 3), swap(third[2:], "col", X * 1)
    parts = [near, first, low, high, third]
    return parts + [swap(part, "col", CORE) for part in parts]


def scatter_col(keep, send2, send13, send0):
    two, rest, zero = (swap(part, "col", CORE) for part in (send2, send13, send0))
    low, high = local(far_x, [coded(2)] * 2, keep, two)
    low, high = swap(low, "col", X * 3), swap(high, "col", X * 1)
    first, third = local(near_x, [coded(4)] * 2, keep, rest, low, high)
    first, third = swap(first, "col", X * 1), swap(third, "col", X * 3)
    line, *far = local(own_x, [plain(1)] + [coded(1)] * 3, keep, zero, first, third)
    return [line] + [swap(far[d - 1], "col", ZLO * d) for d in (1, 2, 3)]


def reduce_row(near, *far):
    total, code = local(own_y, [plain(2), coded(2)], near, *far)
    (share,) = local(own_row, [plain(2, BF)], total, swap(code, "row", ZHI))
    return [share] + [swap(share, "row", Y * d) for d in (1, 2, 3)]


def slot_of(cols, counts, i, k):
    away = cols[i, 0, k] ^ lax.axis_index("col")
    return jnp.where(k < counts[i], (away % 2) * 16 + away // 2, DEAD)


def block_row(step):
    return step ^ (2 * (lax.axis_index("row") % 4))


def join_panel(panel, *parts):
    at = 0
    for part in parts:
        panel[at : at + part.shape[0]] = part[...]
        at += part.shape[0]
    panel[DEAD] = jnp.zeros(panel.shape[1:], panel.dtype)


def image_rows(cols, counts, tiles, panel, step):
    i, total = block_row(step), None
    for k in range(tiles.shape[1]):
        part = lax.dot_general(
            panel[slot_of(cols, counts, i, k)], tiles[i, k], (((1,), (1,)), ((), ())), preferred_element_type=F32
        )
        total = part if total is None else total + part
    return total


def forward_two(cols, counts, tiles, *refs):
    far, panel = refs[10:]
    join_panel(panel, *refs[:10])
    encode([image_rows(cols, counts, tiles, panel, step) for step in (4, 5)], far)


def forward_one(cols, counts, tiles, panel, far):
    encode([image_rows(cols, counts, tiles, panel, step) for step in (2, 3)], far)


def forward_three(cols, counts, tiles, panel, far):
    encode([image_rows(cols, counts, tiles, panel, step) for step in (6, 7)], far)


def forward_near(cols, counts, tiles, panel, near):
    near[0] = image_rows(cols, counts, tiles, panel, 0)
    near[1] = image_rows(cols, counts, tiles, panel, 1)


def sweep_call(kernel, quarter, cols, counts, tiles, operands, outs, aliases=()):
    vmem, smem = pl.BlockSpec(memory_space=pltpu.VMEM), pl.BlockSpec(memory_space=pltpu.SMEM)
    return pl.pallas_call(
        kernel,
        in_specs=[smem, smem] + [vmem] * (1 + len(operands)),
        out_specs=[vmem] * len(outs),
        out_shape=outs,
        input_output_aliases=dict(aliases),
        compiler_params=pltpu.CompilerParams(vmem_limit_bytes=8 << 20),
        cost_estimate=pl.CostEstimate(
            flops=quarter * 32 * 256 * 256 * 128, bytes_accessed=quarter << 20, transcendentals=0
        ),
        name=kernel.__name__,
    )(cols, counts, tiles, *operands)


def forward(cols, counts, tiles, parts):
    two, panel = sweep_call(forward_two, 1, cols, counts, tiles, parts, [coded(2), plain(DEAD + 1, BF)])
    two = swap(two, "row", Y * 2)
    (one,) = sweep_call(forward_one, 16, cols, counts, tiles, [panel], [coded(2)])
    one = swap(one, "row", Y * 1)
    (three,) = sweep_call(forward_three, 16, cols, counts, tiles, [panel], [coded(2)])
    three = swap(three, "row", Y * 3)
    (near,) = sweep_call(forward_near, 0, cols, counts, tiles, [panel], [plain(2)])
    return near, one, two, three


def add_rows(cols, counts, tiles, image, total, distance):
    for half in (0, 1):
        i = block_row(2 * distance + half)
        for k in range(tiles.shape[1]):
            total[slot_of(cols, counts, i, k)] += jnp.dot(image[half], tiles[i, k], preferred_element_type=F32)


def backward_near(cols, counts, tiles, image, total):
    total[...] = jnp.zeros(total.shape, total.dtype)
    add_rows(cols, counts, tiles, image, total, 0)


def backward_three(cols, counts, tiles, before, image, total):
    add_rows(cols, counts, tiles, image, total, 3)


def backward_two(cols, counts, tiles, before, image, total):
    add_rows(cols, counts, tiles, image, total, 2)


def backward_one(cols, counts, tiles, before, image, keep, send2, send13, send0, total):
    add_rows(cols, counts, tiles, image, total, 1)
    keep[...] = total[0:16]
    send0[...] = total[16:20]
    send13[0:4] = total[20:24]
    send2[...] = total[24:28]
    send13[4:8] = total[28:32]


def backward(cols, counts, tiles, image):
    whole = plain(DEAD + 1)
    (total,) = sweep_call(backward_near, 1, cols, counts, tiles, [image[0]], [whole])
    (total,) = sweep_call(backward_three, 1, cols, counts, tiles, [total, image[3]], [whole], [(3, 0)])
    (total,) = sweep_call(backward_two, 1, cols, counts, tiles, [total, image[2]], [whole], [(3, 0)])
    outs = [plain(16), plain(4), plain(8), plain(4), whole]
    return sweep_call(backward_one, 1, cols, counts, tiles, [total, image[1]], outs, [(3, 4)])[:4]


def all_sum(total):
    total = total + swap(total, "col", CORE)
    for axis, bits in (("col", X), ("col", ZLO), ("row", Y)):
        one, two, three = (swap(total, axis, bits * d) for d in (1, 2, 3))
        total = (total + one) + (two + three)
    return total + swap(total, "row", ZHI)


def basis_kernel(gram, result, out, *, factor):
    n, step = gram.shape[0], 16
    row = lax.broadcasted_iota(jnp.int32, (n, n), 0)
    lane = lax.broadcasted_iota(jnp.int32, (n, n), 1)
    left = jnp.concatenate([gram[...], jnp.where(row == lane, 1.0, 0.0)], axis=1)
    row, lane = row[:step], lane[:step]
    inverse = []
    for at in range(0, n, step):
        upper, lower = left[at : at + step, :n], left[at : at + step, n:]
        columns = [jnp.broadcast_to(upper[:, at + c : at + c + 1], (step, n)) for c in range(step)]
        pivots = jnp.zeros((step, n), F32)
        for j in range(step):
            pivot = 1.0 / columns[j][j : j + 1]
            ratio = jnp.where(row > j, columns[j] * pivot, 0.0)
            for c in range(j + 1, step):
                columns[c] = columns[c] - ratio * columns[c][j : j + 1]
            upper = upper - ratio * upper[j : j + 1]
            lower = lower - ratio * lower[j : j + 1]
            pivots = jnp.where(row == j, pivot, pivots)
        inverse.append(lower * (jnp.sqrt(pivots) * factor))
        if at + step < n:
            ratio = jnp.where(lane >= at + step, upper * pivots, 0.0)
            left = left - lax.dot_general(
                ratio,
                jnp.concatenate([upper, lower], axis=1),
                (((0,), (0,)), ((), ())),
                precision=HIGHEST,
                preferred_element_type=F32,
            )
    inverse = jnp.concatenate(inverse, axis=0)
    out[...] = jnp.dot(inverse, result[0], precision=HIGHEST, preferred_element_type=F32).T


def flip(rows, piece):
    piece[0] = rows[...].T


def touch(blocks, token):
    token[...] = jnp.zeros(token.shape, token.dtype)


def body(blocks, block_cols, counts, random_start_panel):
    counts = counts.reshape(-1)
    tiles = blocks[:, 0]
    (token,) = local(touch, [jax.ShapeDtypeStruct((8, 128), F32)], tiles)
    (piece,) = local(flip, [plain(1, BF)], random_start_panel)
    parts = gather_col(piece, token)
    for sweep in range(ITERS):
        image = reduce_row(*forward(block_cols, counts, tiles, parts))
        line = scatter_col(*backward(block_cols, counts, tiles, image))
        if sweep + 1 < ITERS:
            (piece,) = local(own_line, [plain(1, BF)], *line)
            parts = gather_col(piece)
    feature, width = line[0].shape[1:]
    result, gram = local(last_line, [plain(1), jax.ShapeDtypeStruct((feature, feature), F32)], *line)
    nodes = lax.axis_size("row") * lax.axis_size("col") * width

    def basis(*refs):
        basis_kernel(*refs, factor=math.sqrt(nodes))

    return local(basis, [jax.ShapeDtypeStruct((width, feature), F32)], all_sum(gram), result)[0]


def solution(mesh):
    return jax.shard_map(
        body,
        mesh=mesh,
        in_specs=(
            P("col", "row", None, None, None),
            P("col", "row", None),
            P("col", "row"),
            P(("row", "col"), None),
        ),
        out_specs=P(("row", "col"), None),
        check_vma=False,
    )
```

```python
import functools
import math

import jax
import jax.numpy as jnp
from jax import lax
from jax.experimental import pallas as pl
from jax.experimental.pallas import tpu as pltpu
from jax.sharding import PartitionSpec as P

ITERS = 2
CORE, ZLO, X = 1, 2, 8
Y, ZHI = 1, 4
DEAD = 32
TAIL = 16
STEPS = 32000.0
LEAST = 1e-30
BF, F32 = jnp.bfloat16, jnp.float32
HIGHEST = lax.Precision.HIGHEST


def swap(value, axis, bits):
    size = lax.axis_size(axis)
    return lax.ppermute(value, axis, [(i, i ^ bits) for i in range(size)])


def encode(parts, ref):
    top = functools.reduce(jnp.maximum, [jnp.abs(part) for part in parts])
    top = jnp.maximum(jnp.max(top, axis=(0, 1), keepdims=True), LEAST)
    power = jnp.ceil(jnp.log2(top))
    scale = jnp.exp2(-power)
    high = parts[0].shape[0]
    for n, part in enumerate(parts):
        root = part * scale
        root = root * lax.rsqrt(jnp.abs(root) + LEAST)
        root = root * lax.rsqrt(jnp.abs(root) + LEAST)
        ref[n * high : (n + 1) * high] = jnp.round(root * STEPS).astype(jnp.int32).astype(jnp.int16)
    tail = jnp.broadcast_to(power, (TAIL, ref.shape[1]))
    ref[len(parts) * high :] = tail.astype(jnp.int32).astype(jnp.int16)


def decode(ref, high=128):
    count = (ref.shape[0] - TAIL) // high
    gain = jnp.exp2(ref[count * high :].astype(jnp.int32).astype(F32))[:1]
    parts = []
    for n in range(count):
        root = ref[n * high : (n + 1) * high].astype(jnp.int32).astype(F32) * (1.0 / STEPS)
        root = root * jnp.abs(root)
        parts.append(root * jnp.abs(root) * gain)
    return parts


def coded(count, feature=128, width=256):
    return jax.ShapeDtypeStruct((count * feature + TAIL, width), jnp.int16)


def plain(count, dtype=F32, feature=128, width=256):
    return jax.ShapeDtypeStruct((count, feature, width), dtype)


def local(kernel, outs, *args, scratch=(), limit=8):
    vmem = pl.BlockSpec(memory_space=pltpu.VMEM)
    return pl.pallas_call(
        kernel,
        in_specs=[vmem] * len(args),
        out_specs=[vmem] * len(outs),
        out_shape=outs,
        scratch_shapes=scratch,
        compiler_params=pltpu.CompilerParams(vmem_limit_bytes=limit << 20),
        cost_estimate=pl.CostEstimate(flops=1 << 20, bytes_accessed=1 << 20, transcendentals=0),
        name=kernel.__name__,
    )(*args)


def far_x(keep, other, low, high):
    other = decode(other)
    encode([keep[8 + n] + other[n] for n in (0, 1)], low)
    encode([keep[8 + n] + other[n] for n in (2, 3)], high)


def near_x(keep, other, low, high, first, third):
    low, high = decode(low), decode(high)
    one = [keep[4 + n] + other[n] for n in range(4)]
    encode([one[0] + low[0], one[1] + low[1], one[2], one[3]], first)
    three = [keep[12 + n] + other[4 + n] for n in range(4)]
    encode([three[0], three[1], three[2] + high[0], three[3] + high[1]], third)


def own_x(keep, other, first, third, line, *far):
    first, third = decode(first), decode(third)
    total = [keep[n] + other[n] + (first[n] + third[n]) for n in range(4)]
    line[0] = total[0]
    for n in (1, 2, 3):
        encode([total[n]], far[n - 1])


def own_line(line, one, two, three, piece):
    piece[0] = (line[0] + (decode(one)[0] + decode(two)[0] + decode(three)[0])).astype(BF)


def last_line(line, one, two, three, result, gram):
    total = line[0] + (decode(one)[0] + decode(two)[0] + decode(three)[0])
    result[0] = total
    gram[...] = lax.dot_general(
        total, total, (((1,), (1,)), ((), ())), precision=HIGHEST, preferred_element_type=F32
    )


def own_y(near, one, two, three, total, far):
    parts = [decode(ref) for ref in (one, two, three)]
    sums = [near[n] + (parts[0][n] + parts[1][n] + parts[2][n]) for n in (0, 1)]
    total[0], total[1] = sums
    encode(sums, far)


def own_row(total, far, image):
    far = decode(far)
    for n in (0, 1):
        image[n] = (total[n] + far[n]).astype(BF)


def join(a, b, c, d, *refs):
    for n, ref in enumerate((a, b, c, d)):
        refs[-1][n] = ref[0]


def gather_col(piece, *after):
    line = [piece] + [swap(piece, "col", ZLO * d) for d in (1, 2, 3)]
    (near,) = local(join, [plain(4, BF)], *line, *after)
    first, third = swap(near, "col", X * 1), swap(near, "col", X * 3)
    low, high = swap(first[:2], "col", X * 3), swap(third[2:], "col", X * 1)
    parts = [near, first, low, high, third]
    return parts + [swap(part, "col", CORE) for part in parts]


def scatter_col(keep, send2, send13, send0):
    two, rest, zero = (swap(part, "col", CORE) for part in (send2, send13, send0))
    low, high = local(far_x, [coded(2)] * 2, keep, two)
    low, high = swap(low, "col", X * 3), swap(high, "col", X * 1)
    first, third = local(near_x, [coded(4)] * 2, keep, rest, low, high)
    first, third = swap(first, "col", X * 1), swap(third, "col", X * 3)
    line, *far = local(own_x, [plain(1)] + [coded(1)] * 3, keep, zero, first, third)
    return [line] + [swap(far[d - 1], "col", ZLO * d) for d in (1, 2, 3)]


def reduce_row(near, *far):
    total, code = local(own_y, [plain(2), coded(2)], near, *far)
    (share,) = local(own_row, [plain(2, BF)], total, swap(code, "row", ZHI))
    return [share] + [swap(share, "row", Y * d) for d in (1, 2, 3)]


def slot_of(cols, counts, i, k):
    away = cols[i, 0, k] ^ lax.axis_index("col")
    return jnp.where(k < counts[i], (away % 2) * 16 + away // 2, DEAD)


def block_row(step):
    return step ^ (2 * (lax.axis_index("row") % 4))


def join_panel(near, first, third, near_other, first_other, third_other, panel):
    for at, own in ((0, (near, first, third)), (16, (near_other, first_other, third_other))):
        for distance, part in zip((0, 1, 3), own):
            panel[at + 4 * distance : at + 4 * distance + 4] = part[...]
    panel[DEAD] = jnp.zeros(panel.shape[1:], panel.dtype)


def image_rows(cols, counts, tiles, panel, step):
    i, total = block_row(step), None
    for k in range(tiles.shape[1]):
        part = lax.dot_general(
            panel[slot_of(cols, counts, i, k)], tiles[i, k], (((1,), (1,)), ((), ())), preferred_element_type=F32
        )
        total = part if total is None else total + part
    return total


def forward_far(cols, counts, tiles, before, low, high, low_other, high_other, one, two, three, panel):
    for at, part in ((8, low), (10, high), (24, low_other), (26, high_other)):
        panel[at : at + 2] = part[...]
    for distance, far in ((2, two), (1, one), (3, three)):
        encode([image_rows(cols, counts, tiles, panel, 2 * distance + half) for half in (0, 1)], far)


def forward_near(cols, counts, tiles, panel, near):
    near[0] = image_rows(cols, counts, tiles, panel, 0)
    near[1] = image_rows(cols, counts, tiles, panel, 1)


def sweep_call(kernel, quarter, cols, counts, tiles, operands, outs, aliases=()):
    vmem, smem = pl.BlockSpec(memory_space=pltpu.VMEM), pl.BlockSpec(memory_space=pltpu.SMEM)
    return pl.pallas_call(
        kernel,
        in_specs=[smem, smem] + [vmem] * (1 + len(operands)),
        out_specs=[vmem] * len(outs),
        out_shape=outs,
        input_output_aliases=dict(aliases),
        compiler_params=pltpu.CompilerParams(vmem_limit_bytes=8 << 20),
        cost_estimate=pl.CostEstimate(
            flops=quarter * 32 * 256 * 256 * 128, bytes_accessed=quarter << 20, transcendentals=0
        ),
        name=kernel.__name__,
    )(cols, counts, tiles, *operands)


def forward(cols, counts, tiles, parts):
    near, first, low, high, third = parts[:5]
    others = parts[5:]
    (panel,) = local(join_panel, [plain(DEAD + 1, BF)], near, first, third, others[0], others[1], others[4])
    outs = [coded(2)] * 3 + [plain(DEAD + 1, BF)]
    *far, panel = sweep_call(
        forward_far, 3, cols, counts, tiles, [panel, low, high, others[2], others[3]], outs, [(3, 3)]
    )
    far = [swap(far[d - 1], "row", Y * d) for d in (1, 2, 3)]
    (near,) = sweep_call(forward_near, 1, cols, counts, tiles, [panel], [plain(2)])
    return near, *far


def add_rows(cols, counts, tiles, image, total, distance):
    for half in (0, 1):
        i = block_row(2 * distance + half)
        for k in range(tiles.shape[1]):
            total[slot_of(cols, counts, i, k)] += jnp.dot(image[half], tiles[i, k], preferred_element_type=F32)


def backward_near(cols, counts, tiles, image, total):
    total[...] = jnp.zeros(total.shape, total.dtype)
    add_rows(cols, counts, tiles, image, total, 0)


def backward_three(cols, counts, tiles, before, image, total):
    add_rows(cols, counts, tiles, image, total, 3)


def backward_two(cols, counts, tiles, before, image, total):
    add_rows(cols, counts, tiles, image, total, 2)


def backward_one(cols, counts, tiles, before, image, keep, send2, send13, send0, total):
    add_rows(cols, counts, tiles, image, total, 1)
    keep[...] = total[0:16]
    send0[...] = total[16:20]
    send13[0:4] = total[20:24]
    encode([total[24 + n] for n in range(4)], send2)
    send13[4:8] = total[28:32]


def backward(cols, counts, tiles, image):
    whole = plain(DEAD + 1)
    (total,) = sweep_call(backward_near, 1, cols, counts, tiles, [image[0]], [whole])
    (total,) = sweep_call(backward_three, 1, cols, counts, tiles, [total, image[3]], [whole], [(3, 0)])
    (total,) = sweep_call(backward_two, 1, cols, counts, tiles, [total, image[2]], [whole], [(3, 0)])
    outs = [plain(16), coded(4), plain(8), plain(4), whole]
    return sweep_call(backward_one, 1, cols, counts, tiles, [total, image[1]], outs, [(3, 4)])[:4]


def all_sum(total):
    total = total + swap(total, "col", CORE)
    for axis, bits in (("col", X), ("col", ZLO), ("row", Y)):
        one, two, three = (swap(total, axis, bits * d) for d in (1, 2, 3))
        total = (total + one) + (two + three)
    return total + swap(total, "row", ZHI)


def basis_kernel(gram, result, out, *, factor):
    n, step = gram.shape[0], 16
    row = lax.broadcasted_iota(jnp.int32, (n, n), 0)
    lane = lax.broadcasted_iota(jnp.int32, (n, n), 1)
    left = jnp.concatenate([gram[...], jnp.where(row == lane, 1.0, 0.0)], axis=1)
    row, lane = row[:step], lane[:step]
    inverse = []
    for at in range(0, n, step):
        upper, lower = left[at : at + step, :n], left[at : at + step, n:]
        columns = [jnp.broadcast_to(upper[:, at + c : at + c + 1], (step, n)) for c in range(step)]
        pivots = jnp.zeros((step, n), F32)
        for j in range(step):
            pivot = 1.0 / columns[j][j : j + 1]
            ratio = jnp.where(row > j, columns[j] * pivot, 0.0)
            for c in range(j + 1, step):
                columns[c] = columns[c] - ratio * columns[c][j : j + 1]
            upper = upper - ratio * upper[j : j + 1]
            lower = lower - ratio * lower[j : j + 1]
            pivots = jnp.where(row == j, pivot, pivots)
        inverse.append(lower * (jnp.sqrt(pivots) * factor))
        if at + step < n:
            ratio = jnp.where(lane >= at + step, upper * pivots, 0.0)
            left = left - lax.dot_general(
                ratio,
                jnp.concatenate([upper, lower], axis=1),
                (((0,), (0,)), ((), ())),
                precision=HIGHEST,
                preferred_element_type=F32,
            )
    inverse = jnp.concatenate(inverse, axis=0)
    out[...] = jnp.dot(inverse, result[0], precision=HIGHEST, preferred_element_type=F32).T


def flip(rows, piece):
    piece[0] = rows[...].T


def touch(blocks, token):
    token[...] = jnp.zeros(token.shape, token.dtype)


def body(blocks, block_cols, counts, random_start_panel):
    counts = counts.reshape(-1)
    tiles = blocks[:, 0]
    (token,) = local(touch, [jax.ShapeDtypeStruct((8, 128), F32)], tiles)
    (piece,) = local(flip, [plain(1, BF)], random_start_panel)
    parts = gather_col(piece, token)
    for sweep in range(ITERS):
        image = reduce_row(*forward(block_cols, counts, tiles, parts))
        line = scatter_col(*backward(block_cols, counts, tiles, image))
        if sweep + 1 < ITERS:
            (piece,) = local(own_line, [plain(1, BF)], *line)
            parts = gather_col(piece)
    feature, width = line[0].shape[1:]
    result, gram = local(last_line, [plain(1), jax.ShapeDtypeStruct((feature, feature), F32)], *line)
    nodes = lax.axis_size("row") * lax.axis_size("col") * width

    def basis(*refs):
        basis_kernel(*refs, factor=math.sqrt(nodes))

    return local(basis, [jax.ShapeDtypeStruct((width, feature), F32)], all_sum(gram), result)[0]


def solution(mesh):
    return jax.shard_map(
        body,
        mesh=mesh,
        in_specs=(
            P("col", "row", None, None, None),
            P("col", "row", None),
            P("col", "row"),
            P(("row", "col"), None),
        ),
        out_specs=P(("row", "col"), None),
        check_vma=False,
    )
```

```python
import functools
import math

import jax
import jax.numpy as jnp
from jax import lax
from jax.experimental import pallas as pl
from jax.experimental.pallas import tpu as pltpu
from jax.sharding import PartitionSpec as P

ITERS = 2
CORE, ZLO, X = 1, 2, 8
Y, ZHI = 1, 4
DEAD = 32
TAIL = 16
STEPS = 32000.0
LEAST = 1e-30
BF, F32 = jnp.bfloat16, jnp.float32
HIGHEST = lax.Precision.HIGHEST


def swap(value, axis, bits):
    size = lax.axis_size(axis)
    return lax.ppermute(value, axis, [(i, i ^ bits) for i in range(size)])


def encode(parts, ref):
    top = functools.reduce(jnp.maximum, [jnp.abs(part) for part in parts])
    top = jnp.maximum(jnp.max(top, axis=(0, 1), keepdims=True), LEAST)
    power = jnp.ceil(jnp.log2(top))
    scale = jnp.exp2(-power)
    high = parts[0].shape[0]
    for n, part in enumerate(parts):
        root = part * scale
        root = root * lax.rsqrt(jnp.abs(root) + LEAST)
        root = root * lax.rsqrt(jnp.abs(root) + LEAST)
        ref[n * high : (n + 1) * high] = jnp.round(root * STEPS).astype(jnp.int32).astype(jnp.int16)
    tail = jnp.broadcast_to(power, (TAIL, ref.shape[1]))
    ref[len(parts) * high :] = tail.astype(jnp.int32).astype(jnp.int16)


def decode(ref, high=128):
    count = (ref.shape[0] - TAIL) // high
    gain = jnp.exp2(ref[count * high :].astype(jnp.int32).astype(F32))[:1]
    parts = []
    for n in range(count):
        root = ref[n * high : (n + 1) * high].astype(jnp.int32).astype(F32) * (1.0 / STEPS)
        root = root * jnp.abs(root)
        parts.append(root * jnp.abs(root) * gain)
    return parts


def coded(count, feature=128, width=256):
    return jax.ShapeDtypeStruct((count * feature + TAIL, width), jnp.int16)


def plain(count, dtype=F32, feature=128, width=256):
    return jax.ShapeDtypeStruct((count, feature, width), dtype)


def local(kernel, outs, *args, scratch=(), limit=8):
    vmem = pl.BlockSpec(memory_space=pltpu.VMEM)
    return pl.pallas_call(
        kernel,
        in_specs=[vmem] * len(args),
        out_specs=[vmem] * len(outs),
        out_shape=outs,
        scratch_shapes=scratch,
        compiler_params=pltpu.CompilerParams(vmem_limit_bytes=limit << 20),
        cost_estimate=pl.CostEstimate(flops=1 << 20, bytes_accessed=1 << 20, transcendentals=0),
        name=kernel.__name__,
    )(*args)


def far_x(keep, other, low, high):
    encode([keep[8 + n] + other[n] for n in (0, 1)], low)
    encode([keep[8 + n] + other[n] for n in (2, 3)], high)


def near_x(keep, other, low, high, first, third):
    low, high = decode(low), decode(high)
    one = [keep[4 + n] + other[n] for n in range(4)]
    encode([one[0] + low[0], one[1] + low[1], one[2], one[3]], first)
    three = [keep[12 + n] + other[4 + n] for n in range(4)]
    encode([three[0], three[1], three[2] + high[0], three[3] + high[1]], third)


def own_x(keep, other, first, third, line, *far):
    first, third = decode(first), decode(third)
    total = [keep[n] + other[n] + (first[n] + third[n]) for n in range(4)]
    line[0] = total[0]
    for n in (1, 2, 3):
        encode([total[n]], far[n - 1])


def own_line(line, one, two, three, piece):
    piece[0] = (line[0] + (decode(one)[0] + decode(two)[0] + decode(three)[0])).astype(BF)


def last_line(line, one, two, three, result, gram):
    total = line[0] + (decode(one)[0] + decode(two)[0] + decode(three)[0])
    result[0] = total
    gram[...] = lax.dot_general(
        total, total, (((1,), (1,)), ((), ())), precision=HIGHEST, preferred_element_type=F32
    )


def own_y(near, one, two, three, total, far):
    parts = [decode(ref) for ref in (one, two, three)]
    sums = [near[n] + (parts[0][n] + parts[1][n] + parts[2][n]) for n in (0, 1)]
    total[0], total[1] = sums
    encode(sums, far)


def own_row(total, far, image):
    far = decode(far)
    for n in (0, 1):
        image[n] = (total[n] + far[n]).astype(BF)


def join(a, b, c, d, *refs):
    for n, ref in enumerate((a, b, c, d)):
        refs[-1][n] = ref[0]


def gather_col(piece, *after):
    line = [piece] + [swap(piece, "col", ZLO * d) for d in (1, 2, 3)]
    (near,) = local(join, [plain(4, BF)], *line, *after)
    first, third = swap(near, "col", X * 1), swap(near, "col", X * 3)
    low, high = swap(first[:2], "col", X * 3), swap(third[2:], "col", X * 1)
    parts = [near, first, low, high, third]
    return parts + [swap(part, "col", CORE) for part in parts]


def scatter_col(keep, send2, send13, send0):
    two, rest, zero = (swap(part, "col", CORE) for part in (send2, send13, send0))
    low, high = local(far_x, [coded(2)] * 2, keep, two)
    low, high = swap(low, "col", X * 3), swap(high, "col", X * 1)
    first, third = local(near_x, [coded(4)] * 2, keep, rest, low, high)
    first, third = swap(first, "col", X * 1), swap(third, "col", X * 3)
    line, *far = local(own_x, [plain(1)] + [coded(1)] * 3, keep, zero, first, third)
    return [line] + [swap(far[d - 1], "col", ZLO * d) for d in (1, 2, 3)]


def reduce_row(near, *far):
    total, code = local(own_y, [plain(2), coded(2)], near, *far)
    (share,) = local(own_row, [plain(2, BF)], total, swap(code, "row", ZHI))
    one, three, two = (swap(share, "row", Y * d) for d in (1, 3, 2))
    return share, one, two, three


def slot_of(cols, counts, i, k):
    away = cols[i, 0, k] ^ lax.axis_index("col")
    return jnp.where(k < counts[i], (away % 2) * 16 + away // 2, DEAD)


def block_row(step):
    return step ^ (2 * (lax.axis_index("row") % 4))


def join_panel(near, first, third, near_other, first_other, third_other, panel):
    for at, own in ((0, (near, first, third)), (16, (near_other, first_other, third_other))):
        for distance, part in zip((0, 1, 3), own):
            panel[at + 4 * distance : at + 4 * distance + 4] = part[...]
    panel[DEAD] = jnp.zeros(panel.shape[1:], panel.dtype)


def image_rows(cols, counts, tiles, panel, step):
    i, total = block_row(step), None
    for k in range(tiles.shape[1]):
        part = lax.dot_general(
            panel[slot_of(cols, counts, i, k)], tiles[i, k], (((1,), (1,)), ((), ())), preferred_element_type=F32
        )
        total = part if total is None else total + part
    return total


def forward_far(cols, counts, tiles, before, low, high, low_other, high_other, one, two, three, panel):
    for at, part in ((8, low), (10, high), (24, low_other), (26, high_other)):
        panel[at : at + 2] = part[...]
    for distance, far in ((2, two), (1, one), (3, three)):
        encode([image_rows(cols, counts, tiles, panel, 2 * distance + half) for half in (0, 1)], far)


def forward_near(cols, counts, tiles, panel, near):
    near[0] = image_rows(cols, counts, tiles, panel, 0)
    near[1] = image_rows(cols, counts, tiles, panel, 1)


def sweep_call(kernel, quarter, cols, counts, tiles, operands, outs, aliases=()):
    vmem, smem = pl.BlockSpec(memory_space=pltpu.VMEM), pl.BlockSpec(memory_space=pltpu.SMEM)
    return pl.pallas_call(
        kernel,
        in_specs=[smem, smem] + [vmem] * (1 + len(operands)),
        out_specs=[vmem] * len(outs),
        out_shape=outs,
        input_output_aliases=dict(aliases),
        compiler_params=pltpu.CompilerParams(vmem_limit_bytes=8 << 20),
        cost_estimate=pl.CostEstimate(
            flops=quarter * 32 * 256 * 256 * 128, bytes_accessed=quarter << 20, transcendentals=0
        ),
        name=kernel.__name__,
    )(cols, counts, tiles, *operands)


def forward(cols, counts, tiles, parts):
    near, first, low, high, third = parts[:5]
    others = parts[5:]
    (panel,) = local(join_panel, [plain(DEAD + 1, BF)], near, first, third, others[0], others[1], others[4])
    outs = [coded(2)] * 3 + [plain(DEAD + 1, BF)]
    *far, panel = sweep_call(
        forward_far, 3, cols, counts, tiles, [panel, low, high, others[2], others[3]], outs, [(3, 3)]
    )
    far = [swap(far[d - 1], "row", Y * d) for d in (1, 3, 2)]
    (near,) = sweep_call(forward_near, 1, cols, counts, tiles, [panel], [plain(2)])
    return near, *far


def add_rows(cols, counts, tiles, image, total, distance):
    for half in (0, 1):
        i = block_row(2 * distance + half)
        for k in range(tiles.shape[1]):
            total[slot_of(cols, counts, i, k)] += jnp.dot(image[half], tiles[i, k], preferred_element_type=F32)


def backward_near(cols, counts, tiles, image, total):
    total[...] = jnp.zeros(total.shape, total.dtype)
    add_rows(cols, counts, tiles, image, total, 0)


def backward_three(cols, counts, tiles, before, image, total):
    add_rows(cols, counts, tiles, image, total, 3)


def backward_one(cols, counts, tiles, before, image, total):
    add_rows(cols, counts, tiles, image, total, 1)


def backward_two(cols, counts, tiles, before, image, keep, send2, send13, send0, total):
    add_rows(cols, counts, tiles, image, total, 2)
    keep[...] = total[0:16]
    send0[...] = total[16:20]
    send13[0:4] = total[20:24]
    send2[...] = total[24:28]
    send13[4:8] = total[28:32]


def backward(cols, counts, tiles, image):
    whole = plain(DEAD + 1)
    (total,) = sweep_call(backward_near, 1, cols, counts, tiles, [image[0]], [whole])
    (total,) = sweep_call(backward_one, 1, cols, counts, tiles, [total, image[1]], [whole], [(3, 0)])
    (total,) = sweep_call(backward_three, 1, cols, counts, tiles, [total, image[3]], [whole], [(3, 0)])
    outs = [plain(16), plain(4), plain(8), plain(4), whole]
    return sweep_call(backward_two, 1, cols, counts, tiles, [total, image[2]], outs, [(3, 4)])[:4]


def all_sum(total):
    total = total + swap(total, "col", CORE)
    for axis, bits in (("col", X), ("col", ZLO), ("row", Y)):
        one, two, three = (swap(total, axis, bits * d) for d in (1, 2, 3))
        total = (total + one) + (two + three)
    return total + swap(total, "row", ZHI)


def basis_kernel(gram, result, out, *, factor):
    n, step = gram.shape[0], 16
    row = lax.broadcasted_iota(jnp.int32, (n, n), 0)
    lane = lax.broadcasted_iota(jnp.int32, (n, n), 1)
    left = jnp.concatenate([gram[...], jnp.where(row == lane, 1.0, 0.0)], axis=1)
    row, lane = row[:step], lane[:step]
    inverse = []
    for at in range(0, n, step):
        upper, lower = left[at : at + step, :n], left[at : at + step, n:]
        columns = [jnp.broadcast_to(upper[:, at + c : at + c + 1], (step, n)) for c in range(step)]
        pivots = jnp.zeros((step, n), F32)
        for j in range(step):
            pivot = 1.0 / columns[j][j : j + 1]
            ratio = jnp.where(row > j, columns[j] * pivot, 0.0)
            for c in range(j + 1, step):
                columns[c] = columns[c] - ratio * columns[c][j : j + 1]
            upper = upper - ratio * upper[j : j + 1]
            lower = lower - ratio * lower[j : j + 1]
            pivots = jnp.where(row == j, pivot, pivots)
        inverse.append(lower * (jnp.sqrt(pivots) * factor))
        if at + step < n:
            ratio = jnp.where(lane >= at + step, upper * pivots, 0.0)
            left = left - lax.dot_general(
                ratio,
                jnp.concatenate([upper, lower], axis=1),
                (((0,), (0,)), ((), ())),
                precision=HIGHEST,
                preferred_element_type=F32,
            )
    inverse = jnp.concatenate(inverse, axis=0)
    out[...] = jnp.dot(inverse, result[0], precision=HIGHEST, preferred_element_type=F32).T


def flip(rows, piece):
    piece[0] = rows[...].T


def touch(blocks, token):
    token[...] = jnp.zeros(token.shape, token.dtype)


def body(blocks, block_cols, counts, random_start_panel):
    counts = counts.reshape(-1)
    tiles = blocks[:, 0]
    (token,) = local(touch, [jax.ShapeDtypeStruct((8, 128), F32)], tiles)
    (piece,) = local(flip, [plain(1, BF)], random_start_panel)
    parts = gather_col(piece, token)
    for sweep in range(ITERS):
        image = reduce_row(*forward(block_cols, counts, tiles, parts))
        line = scatter_col(*backward(block_cols, counts, tiles, image))
        if sweep + 1 < ITERS:
            (piece,) = local(own_line, [plain(1, BF)], *line)
            parts = gather_col(piece)
    feature, width = line[0].shape[1:]
    result, gram = local(last_line, [plain(1), jax.ShapeDtypeStruct((feature, feature), F32)], *line)
    nodes = lax.axis_size("row") * lax.axis_size("col") * width

    def basis(*refs):
        basis_kernel(*refs, factor=math.sqrt(nodes))

    return local(basis, [jax.ShapeDtypeStruct((width, feature), F32)], all_sum(gram), result)[0]


def solution(mesh):
    return jax.shard_map(
        body,
        mesh=mesh,
        in_specs=(
            P("col", "row", None, None, None),
            P("col", "row", None),
            P("col", "row"),
            P(("row", "col"), None),
        ),
        out_specs=P(("row", "col"), None),
        check_vma=False,
    )
```

```python
import functools
import math

import jax
import jax.numpy as jnp
from jax import lax
from jax.experimental import pallas as pl
from jax.experimental.pallas import tpu as pltpu
from jax.sharding import PartitionSpec as P

ITERS = 2
CORE, ZLO, X = 1, 2, 8
Y, ZHI = 1, 4
DEAD = 32
TAIL = 16
STEPS = 32000.0
LEAST = 1e-30
BF, F32 = jnp.bfloat16, jnp.float32
HIGHEST = lax.Precision.HIGHEST


def swap(value, axis, bits):
    size = lax.axis_size(axis)
    return lax.ppermute(value, axis, [(i, i ^ bits) for i in range(size)])


def encode(parts, ref):
    top = functools.reduce(jnp.maximum, [jnp.abs(part) for part in parts])
    top = jnp.maximum(jnp.max(top, axis=(0, 1), keepdims=True), LEAST)
    power = jnp.ceil(jnp.log2(top))
    scale = jnp.exp2(-power)
    high = parts[0].shape[0]
    for n, part in enumerate(parts):
        root = part * scale
        root = root * lax.rsqrt(jnp.abs(root) + LEAST)
        root = root * lax.rsqrt(jnp.abs(root) + LEAST)
        ref[n * high : (n + 1) * high] = jnp.round(root * STEPS).astype(jnp.int32).astype(jnp.int16)
    tail = jnp.broadcast_to(power, (TAIL, ref.shape[1]))
    ref[len(parts) * high :] = tail.astype(jnp.int32).astype(jnp.int16)


def decode(ref, high=128):
    count = (ref.shape[0] - TAIL) // high
    gain = jnp.exp2(ref[count * high :].astype(jnp.int32).astype(F32))[:1]
    parts = []
    for n in range(count):
        root = ref[n * high : (n + 1) * high].astype(jnp.int32).astype(F32) * (1.0 / STEPS)
        root = root * jnp.abs(root)
        parts.append(root * jnp.abs(root) * gain)
    return parts


def coded(count, feature=128, width=256):
    return jax.ShapeDtypeStruct((count * feature + TAIL, width), jnp.int16)


def plain(count, dtype=F32, feature=128, width=256):
    return jax.ShapeDtypeStruct((count, feature, width), dtype)


def local(kernel, outs, *args, scratch=(), limit=8):
    vmem = pl.BlockSpec(memory_space=pltpu.VMEM)
    return pl.pallas_call(
        kernel,
        in_specs=[vmem] * len(args),
        out_specs=[vmem] * len(outs),
        out_shape=outs,
        scratch_shapes=scratch,
        compiler_params=pltpu.CompilerParams(vmem_limit_bytes=limit << 20),
        cost_estimate=pl.CostEstimate(flops=1 << 20, bytes_accessed=1 << 20, transcendentals=0),
        name=kernel.__name__,
    )(*args)


def far_x(keep, other, low, high):
    encode([keep[8 + n] + other[n] for n in (0, 1)], low)
    encode([keep[8 + n] + other[n] for n in (2, 3)], high)


def near_x(keep, other, low, high, first, third):
    low, high = decode(low), decode(high)
    one = [keep[4 + n] + other[n] for n in range(4)]
    encode([one[0] + low[0], one[1] + low[1], one[2], one[3]], first)
    three = [keep[12 + n] + other[4 + n] for n in range(4)]
    encode([three[0], three[1], three[2] + high[0], three[3] + high[1]], third)


def own_x(keep, other, first, third, line, *far):
    first, third = decode(first), decode(third)
    total = [keep[n] + other[n] + (first[n] + third[n]) for n in range(4)]
    line[0] = total[0]
    for n in (1, 2, 3):
        encode([total[n]], far[n - 1])


def own_line(line, one, two, three, piece):
    piece[0] = (line[0] + (decode(one)[0] + decode(two)[0] + decode(three)[0])).astype(BF)


def last_line(line, one, two, three, result, gram):
    total = line[0] + (decode(one)[0] + decode(two)[0] + decode(three)[0])
    result[0] = total
    gram[...] = lax.dot_general(
        total, total, (((1,), (1,)), ((), ())), precision=HIGHEST, preferred_element_type=F32
    )


def own_y(near, one, two, three, total, far):
    parts = [decode(ref) for ref in (one, two, three)]
    sums = [near[n] + (parts[0][n] + parts[1][n] + parts[2][n]) for n in (0, 1)]
    total[0], total[1] = sums
    encode(sums, far)


def own_row(total, far, image):
    far = decode(far)
    for n in (0, 1):
        image[n] = (total[n] + far[n]).astype(BF)


def join(a, b, c, d, *refs):
    for n, ref in enumerate((a, b, c, d)):
        refs[-1][n] = ref[0]


def gather_col(piece, *after):
    line = [piece] + [swap(piece, "col", ZLO * d) for d in (1, 2, 3)]
    (near,) = local(join, [plain(4, BF)], *line, *after)
    first, third = swap(near, "col", X * 1), swap(near, "col", X * 3)
    low, high = swap(first[:2], "col", X * 3), swap(third[2:], "col", X * 1)
    parts = [near, first, low, high, third]
    return parts + [swap(part, "col", CORE) for part in parts]


def scatter_col(keep, send2, send13, send0):
    two, rest, zero = (swap(part, "col", CORE) for part in (send2, send13, send0))
    low, high = local(far_x, [coded(2)] * 2, keep, two)
    low, high = swap(low, "col", X * 3), swap(high, "col", X * 1)
    first, third = local(near_x, [coded(4)] * 2, keep, rest, low, high)
    first, third = swap(first, "col", X * 1), swap(third, "col", X * 3)
    line, *far = local(own_x, [plain(1)] + [coded(1)] * 3, keep, zero, first, third)
    return [line] + [swap(far[d - 1], "col", ZLO * d) for d in (1, 2, 3)]


def reduce_row(near, *far):
    total, code = local(own_y, [plain(2), coded(2)], near, *far)
    (share,) = local(own_row, [plain(2, BF)], total, swap(code, "row", ZHI))
    one, three, two = (swap(share, "row", Y * d) for d in (1, 3, 2))
    return share, one, two, three


def slot_of(cols, counts, i, k):
    away = cols[i, 0, k] ^ lax.axis_index("col")
    return jnp.where(k < counts[i], (away % 2) * 16 + away // 2, DEAD)


def block_row(step):
    return step ^ (2 * (lax.axis_index("row") % 4))


def join_panel(near, first, third, near_other, first_other, third_other, panel):
    for at, own in ((0, (near, first, third)), (16, (near_other, first_other, third_other))):
        for distance, part in zip((0, 1, 3), own):
            panel[at + 4 * distance : at + 4 * distance + 4] = part[...]
    panel[DEAD] = jnp.zeros(panel.shape[1:], panel.dtype)


def image_rows(cols, counts, tiles, panel, step):
    i, total = block_row(step), None
    for k in range(tiles.shape[1]):
        part = lax.dot_general(
            panel[slot_of(cols, counts, i, k)], tiles[i, k], (((1,), (1,)), ((), ())), preferred_element_type=F32
        )
        total = part if total is None else total + part
    return total


def forward_far(cols, counts, tiles, before, low, high, low_other, high_other, one, two, three, panel):
    for at, part in ((8, low), (10, high), (24, low_other), (26, high_other)):
        panel[at : at + 2] = part[...]
    for distance, far in ((2, two), (1, one), (3, three)):
        encode([image_rows(cols, counts, tiles, panel, 2 * distance + half) for half in (0, 1)], far)


def forward_near(cols, counts, tiles, panel, near):
    near[0] = image_rows(cols, counts, tiles, panel, 0)
    near[1] = image_rows(cols, counts, tiles, panel, 1)


def sweep_call(kernel, quarter, cols, counts, tiles, operands, outs, aliases=()):
    vmem, smem = pl.BlockSpec(memory_space=pltpu.VMEM), pl.BlockSpec(memory_space=pltpu.SMEM)
    return pl.pallas_call(
        kernel,
        in_specs=[smem, smem] + [vmem] * (1 + len(operands)),
        out_specs=[vmem] * len(outs),
        out_shape=outs,
        input_output_aliases=dict(aliases),
        compiler_params=pltpu.CompilerParams(vmem_limit_bytes=8 << 20),
        cost_estimate=pl.CostEstimate(
            flops=quarter * 32 * 256 * 256 * 128, bytes_accessed=quarter << 20, transcendentals=0
        ),
        name=kernel.__name__,
    )(cols, counts, tiles, *operands)


def forward(cols, counts, tiles, parts):
    near, first, low, high, third = parts[:5]
    others = parts[5:]
    (panel,) = local(join_panel, [plain(DEAD + 1, BF)], near, first, third, others[0], others[1], others[4])
    outs = [coded(2)] * 3 + [plain(DEAD + 1, BF)]
    *far, panel = sweep_call(
        forward_far, 3, cols, counts, tiles, [panel, low, high, others[2], others[3]], outs, [(3, 3)]
    )
    far = [swap(far[d - 1], "row", Y * d) for d in (1, 3, 2)]
    (near,) = sweep_call(forward_near, 1, cols, counts, tiles, [panel], [plain(2)])
    return near, *far


def add_rows(cols, counts, tiles, image, total, distance):
    for half in (0, 1):
        i = block_row(2 * distance + half)
        for k in range(tiles.shape[1]):
            total[slot_of(cols, counts, i, k)] += jnp.dot(image[half], tiles[i, k], preferred_element_type=F32)


def backward_near(cols, counts, tiles, image, total):
    total[...] = jnp.zeros(total.shape, total.dtype)
    add_rows(cols, counts, tiles, image, total, 0)


def backward_three(cols, counts, tiles, before, image, total):
    add_rows(cols, counts, tiles, image, total, 3)


def backward_one(cols, counts, tiles, before, image, total):
    add_rows(cols, counts, tiles, image, total, 1)


def backward_two(cols, counts, tiles, before, image, keep, send2, send13, send0, total):
    add_rows(cols, counts, tiles, image, total, 2)
    keep[...] = total[0:16]
    send0[...] = total[16:20]
    send13[0:4] = total[20:24]
    send2[...] = total[24:28]
    send13[4:8] = total[28:32]


def backward(cols, counts, tiles, image):
    whole = plain(DEAD + 1)
    (total,) = sweep_call(backward_near, 1, cols, counts, tiles, [image[0]], [whole])
    (total,) = sweep_call(backward_one, 1, cols, counts, tiles, [total, image[1]], [whole], [(3, 0)])
    (total,) = sweep_call(backward_three, 1, cols, counts, tiles, [total, image[3]], [whole], [(3, 0)])
    outs = [plain(16), plain(4), plain(8), plain(4), whole]
    return sweep_call(backward_two, 1, cols, counts, tiles, [total, image[2]], outs, [(3, 4)])[:4]


def all_sum(total):
    total = total + swap(total, "col", CORE)
    for axis, bits, order in (("col", X, (2, 3, 1)), ("col", ZLO, (1, 2, 3)), ("row", Y, (2, 3, 1))):
        got = [swap(total, axis, bits * d) for d in order]
        total = (got[0] + got[1]) + (got[2] + total)
    return total + swap(total, "row", ZHI)


def basis_kernel(gram, result, out, *, factor):
    n, step = gram.shape[0], 32
    row = lax.broadcasted_iota(jnp.int32, (n, n), 0)
    lane = lax.broadcasted_iota(jnp.int32, (n, n), 1)
    left = jnp.concatenate([gram[...], jnp.where(row == lane, 1.0, 0.0)], axis=1)
    row, inverse = row[:step], []
    for at in range(0, n, step):
        upper, lower = left[:step, :n], left[:step, n:]
        columns = [jnp.broadcast_to(upper[:, at + c : at + c + 1], (step, n)) for c in range(step)]
        pivots = jnp.zeros((step, n), F32)
        for j in range(step):
            pivot = 1.0 / columns[j][j : j + 1]
            ratio = jnp.where(row > j, columns[j] * pivot, 0.0)
            for c in range(j + 1, step):
                columns[c] = columns[c] - ratio * columns[c][j : j + 1]
            upper = upper - ratio * upper[j : j + 1]
            lower = lower - ratio * lower[j : j + 1]
            pivots = jnp.where(row == j, pivot, pivots)
        inverse.append(lower * (jnp.sqrt(pivots) * factor))
        if at + step < n:
            left = left[step:] - jnp.dot(
                (upper * pivots).T[at + step :],
                jnp.concatenate([upper, lower], axis=1),
                precision=HIGHEST,
                preferred_element_type=F32,
            )
    inverse = jnp.concatenate(inverse, axis=0)
    out[...] = jnp.dot(inverse, result[0], precision=HIGHEST, preferred_element_type=F32).T


def flip(rows, piece):
    piece[0] = rows[...].T


def touch(blocks, token):
    token[...] = jnp.zeros(token.shape, token.dtype)


def body(blocks, block_cols, counts, random_start_panel):
    counts = counts.reshape(-1)
    tiles = blocks[:, 0]
    (token,) = local(touch, [jax.ShapeDtypeStruct((8, 128), F32)], tiles)
    (piece,) = local(flip, [plain(1, BF)], random_start_panel)
    parts = gather_col(piece, token)
    for sweep in range(ITERS):
        image = reduce_row(*forward(block_cols, counts, tiles, parts))
        line = scatter_col(*backward(block_cols, counts, tiles, image))
        if sweep + 1 < ITERS:
            (piece,) = local(own_line, [plain(1, BF)], *line)
            parts = gather_col(piece)
    feature, width = line[0].shape[1:]
    result, gram = local(last_line, [plain(1), jax.ShapeDtypeStruct((feature, feature), F32)], *line)
    nodes = lax.axis_size("row") * lax.axis_size("col") * width

    def basis(*refs):
        basis_kernel(*refs, factor=math.sqrt(nodes))

    return local(basis, [jax.ShapeDtypeStruct((width, feature), F32)], all_sum(gram), result)[0]


def solution(mesh):
    return jax.shard_map(
        body,
        mesh=mesh,
        in_specs=(
            P("col", "row", None, None, None),
            P("col", "row", None),
            P("col", "row"),
            P(("row", "col"), None),
        ),
        out_specs=P(("row", "col"), None),
        check_vma=False,
    )
```

```python
import functools
import math

import jax
import jax.numpy as jnp
from jax import lax
from jax.experimental import pallas as pl
from jax.experimental.pallas import tpu as pltpu
from jax.sharding import PartitionSpec as P

ITERS = 2
CORE, ZLO, X = 1, 2, 8
Y, ZHI = 1, 4
DEAD = 32
TAIL = 16
STEPS = 32000.0
LEAST = 1e-30
BF, F32 = jnp.bfloat16, jnp.float32
HIGHEST = lax.Precision.HIGHEST


def swap(value, axis, bits):
    size = lax.axis_size(axis)
    return lax.ppermute(value, axis, [(i, i ^ bits) for i in range(size)])


def encode(*pairs):
    top = functools.reduce(jnp.maximum, [jnp.abs(part) for parts, _ in pairs for part in parts])
    top = jnp.maximum(jnp.max(top, axis=(0, 1), keepdims=True), LEAST)
    power = jnp.ceil(jnp.log2(top))
    scale = jnp.exp2(-power)
    for parts, ref in pairs:
        high, at = parts[0].shape[0], 0
        for part in parts:
            root = part * scale
            root = root * lax.rsqrt(jnp.abs(root) + LEAST)
            root = root * lax.rsqrt(jnp.abs(root) + LEAST)
            code = jnp.round(root * STEPS).astype(jnp.int32).astype(jnp.int16)
            for lane in range(0, part.shape[1], 128):
                ref[at : at + high] = code[:, lane : lane + 128]
                at += high
        ref[at:] = jnp.broadcast_to(power, (TAIL, 128)).astype(jnp.int32).astype(jnp.int16)


def decode(ref, high=128):
    count = (ref.shape[0] - TAIL) // (2 * high)
    gain = jnp.exp2(ref[2 * count * high :].astype(jnp.int32).astype(F32))[:1]
    parts = []
    for n in range(count):
        halves = []
        for at in (2 * n * high, (2 * n + 1) * high):
            root = ref[at : at + high].astype(jnp.int32).astype(F32) * (1.0 / STEPS)
            root = root * jnp.abs(root)
            halves.append(root * jnp.abs(root) * gain)
        parts.append(jnp.concatenate(halves, axis=1))
    return parts


def coded(count, feature=128):
    return jax.ShapeDtypeStruct((2 * count * feature + TAIL, 128), jnp.int16)


def plain(count, dtype=F32, feature=128, width=256):
    return jax.ShapeDtypeStruct((count, feature, width), dtype)


def local(kernel, outs, *args, scratch=(), limit=8):
    vmem = pl.BlockSpec(memory_space=pltpu.VMEM)
    return pl.pallas_call(
        kernel,
        in_specs=[vmem] * len(args),
        out_specs=[vmem] * len(outs),
        out_shape=outs,
        scratch_shapes=scratch,
        compiler_params=pltpu.CompilerParams(vmem_limit_bytes=limit << 20),
        cost_estimate=pl.CostEstimate(flops=1 << 20, bytes_accessed=1 << 20, transcendentals=0),
        name=kernel.__name__,
    )(*args)


def far_x(keep, other, low, high):
    two = [keep[8 + n] + other[n] for n in range(4)]
    encode((two[:2], low), (two[2:], high))


def near_x(keep, other, low, high, first, third):
    low, high = decode(low), decode(high)
    one = [keep[4 + n] + other[n] for n in range(4)]
    three = [keep[12 + n] + other[4 + n] for n in range(4)]
    one[:2] = [one[0] + low[0], one[1] + low[1]]
    three[2:] = [three[2] + high[0], three[3] + high[1]]
    encode((one, first), (three, third))


def own_x(keep, other, first, third, line, *far):
    first, third = decode(first), decode(third)
    total = [keep[n] + other[n] + (first[n] + third[n]) for n in range(4)]
    line[0] = total[0]
    encode(*(([total[n]], far[n - 1]) for n in (1, 2, 3)))


def own_line(line, one, two, three, piece):
    piece[0] = (line[0] + (decode(one)[0] + decode(two)[0] + decode(three)[0])).astype(BF)


def last_line(line, one, two, three, result, gram):
    total = line[0] + (decode(one)[0] + decode(two)[0] + decode(three)[0])
    result[0] = total
    gram[...] = lax.dot_general(
        total, total, (((1,), (1,)), ((), ())), precision=HIGHEST, preferred_element_type=F32
    )


def own_y(near, one, two, three, total, far):
    parts = [decode(ref) for ref in (one, two, three)]
    sums = [near[n] + (parts[0][n] + parts[1][n] + parts[2][n]) for n in (0, 1)]
    total[0], total[1] = sums
    encode((sums, far))


def own_row(total, far, image):
    far = decode(far)
    for n in (0, 1):
        image[n] = (total[n] + far[n]).astype(BF)


def join(a, b, c, d, *refs):
    for n, ref in enumerate((a, b, c, d)):
        refs[-1][n] = ref[0]


def gather_col(piece, *after):
    line = [piece] + [swap(piece, "col", ZLO * d) for d in (1, 2, 3)]
    (near,) = local(join, [plain(4, BF)], *line, *after)
    first, third = swap(near, "col", X * 1), swap(near, "col", X * 3)
    low, high = swap(first[:2], "col", X * 3), swap(third[2:], "col", X * 1)
    parts = [near, first, low, high, third]
    return parts + [swap(part, "col", CORE) for part in parts]


def scatter_col(keep, send2, send13, send0):
    two, rest, zero = (swap(part, "col", CORE) for part in (send2, send13, send0))
    low, high = local(far_x, [coded(2)] * 2, keep, two)
    low, high = swap(low, "col", X * 3), swap(high, "col", X * 1)
    first, third = local(near_x, [coded(4)] * 2, keep, rest, low, high)
    first, third = swap(first, "col", X * 1), swap(third, "col", X * 3)
    line, *far = local(own_x, [plain(1)] + [coded(1)] * 3, keep, zero, first, third)
    return [line] + [swap(far[d - 1], "col", ZLO * d) for d in (1, 2, 3)]


def reduce_row(near, *far):
    total, code = local(own_y, [plain(2), coded(2)], near, *far)
    (share,) = local(own_row, [plain(2, BF)], total, swap(code, "row", ZHI))
    one, three, two = (swap(share, "row", Y * d) for d in (1, 3, 2))
    return share, one, two, three


def slot_of(cols, counts, i, k):
    away = cols[i, 0, k] ^ lax.axis_index("col")
    return jnp.where(k < counts[i], (away % 2) * 16 + away // 2, DEAD)


def block_row(step):
    return step ^ (2 * (lax.axis_index("row") % 4))


def join_panel(near, first, third, near_other, first_other, third_other, panel):
    for at, own in ((0, (near, first, third)), (16, (near_other, first_other, third_other))):
        for distance, part in zip((0, 1, 3), own):
            panel[at + 4 * distance : at + 4 * distance + 4] = part[...]
    panel[DEAD] = jnp.zeros(panel.shape[1:], panel.dtype)


def image_rows(cols, counts, tiles, panel, step):
    i, total = block_row(step), None
    for k in range(tiles.shape[1]):
        part = lax.dot_general(
            panel[slot_of(cols, counts, i, k)], tiles[i, k], (((1,), (1,)), ((), ())), preferred_element_type=F32
        )
        total = part if total is None else total + part
    return total


def forward_far(cols, counts, tiles, before, low, high, low_other, high_other, one, two, three, panel):
    for at, part in ((8, low), (10, high), (24, low_other), (26, high_other)):
        panel[at : at + 2] = part[...]
    rows = [image_rows(cols, counts, tiles, panel, step) for step in range(2, 8)]
    encode((rows[:2], one), (rows[2:4], two), (rows[4:], three))


def forward_near(cols, counts, tiles, panel, near):
    near[0] = image_rows(cols, counts, tiles, panel, 0)
    near[1] = image_rows(cols, counts, tiles, panel, 1)


def sweep_call(kernel, quarter, cols, counts, tiles, operands, outs, aliases=()):
    vmem, smem = pl.BlockSpec(memory_space=pltpu.VMEM), pl.BlockSpec(memory_space=pltpu.SMEM)
    return pl.pallas_call(
        kernel,
        in_specs=[smem, smem] + [vmem] * (1 + len(operands)),
        out_specs=[vmem] * len(outs),
        out_shape=outs,
        input_output_aliases=dict(aliases),
        compiler_params=pltpu.CompilerParams(vmem_limit_bytes=8 << 20),
        cost_estimate=pl.CostEstimate(
            flops=quarter * 32 * 256 * 256 * 128, bytes_accessed=quarter << 20, transcendentals=0
        ),
        name=kernel.__name__,
    )(cols, counts, tiles, *operands)


def forward(cols, counts, tiles, parts):
    near, first, low, high, third = parts[:5]
    others = parts[5:]
    (panel,) = local(join_panel, [plain(DEAD + 1, BF)], near, first, third, others[0], others[1], others[4])
    outs = [coded(2)] * 3 + [plain(DEAD + 1, BF)]
    *far, panel = sweep_call(
        forward_far, 3, cols, counts, tiles, [panel, low, high, others[2], others[3]], outs, [(3, 3)]
    )
    far = [swap(far[d - 1], "row", Y * d) for d in (1, 3, 2)]
    (near,) = sweep_call(forward_near, 1, cols, counts, tiles, [panel], [plain(2)])
    return near, *far


def add_rows(cols, counts, tiles, image, total, distance):
    for half in (0, 1):
        i = block_row(2 * distance + half)
        for k in range(tiles.shape[1]):
            total[slot_of(cols, counts, i, k)] += jnp.dot(image[half], tiles[i, k], preferred_element_type=F32)


def backward_near(cols, counts, tiles, image, total):
    total[...] = jnp.zeros(total.shape, total.dtype)
    add_rows(cols, counts, tiles, image, total, 0)


def backward_three(cols, counts, tiles, before, image, total):
    add_rows(cols, counts, tiles, image, total, 3)


def backward_one(cols, counts, tiles, before, image, total):
    add_rows(cols, counts, tiles, image, total, 1)


def backward_two(cols, counts, tiles, before, image, keep, send2, send13, send0, total):
    add_rows(cols, counts, tiles, image, total, 2)
    keep[...] = total[0:16]
    send0[...] = total[16:20]
    send13[0:4] = total[20:24]
    send2[...] = total[24:28]
    send13[4:8] = total[28:32]


def backward(cols, counts, tiles, image):
    whole = plain(DEAD + 1)
    (total,) = sweep_call(backward_near, 1, cols, counts, tiles, [image[0]], [whole])
    (total,) = sweep_call(backward_one, 1, cols, counts, tiles, [total, image[1]], [whole], [(3, 0)])
    (total,) = sweep_call(backward_three, 1, cols, counts, tiles, [total, image[3]], [whole], [(3, 0)])
    outs = [plain(16), plain(4), plain(8), plain(4), whole]
    return sweep_call(backward_two, 1, cols, counts, tiles, [total, image[2]], outs, [(3, 4)])[:4]


def all_sum(total):
    total = total + swap(total, "col", CORE)
    for axis, bits, order in (("col", X, (2, 3, 1)), ("col", ZLO, (1, 2, 3)), ("row", Y, (2, 3, 1))):
        got = [swap(total, axis, bits * d) for d in order]
        total = (got[0] + got[1]) + (got[2] + total)
    return total + swap(total, "row", ZHI)


def basis_kernel(gram, result, out, *, factor):
    n, step = gram.shape[0], 32
    row = lax.broadcasted_iota(jnp.int32, (n, n), 0)
    lane = lax.broadcasted_iota(jnp.int32, (n, n), 1)
    left = jnp.concatenate([gram[...], jnp.where(row == lane, 1.0, 0.0)], axis=1)
    row, inverse = row[:step], []
    for at in range(0, n, step):
        upper, lower = left[:step, :n], left[:step, n:]
        columns = [jnp.broadcast_to(upper[:, at + c : at + c + 1], (step, n)) for c in range(step)]
        pivots = jnp.zeros((step, n), F32)
        for j in range(step):
            pivot = 1.0 / columns[j][j : j + 1]
            ratio = jnp.where(row > j, columns[j] * pivot, 0.0)
            for c in range(j + 1, step):
                columns[c] = columns[c] - ratio * columns[c][j : j + 1]
            upper = upper - ratio * upper[j : j + 1]
            lower = lower - ratio * lower[j : j + 1]
            pivots = jnp.where(row == j, pivot, pivots)
        inverse.append(lower * (jnp.sqrt(pivots) * factor))
        if at + step < n:
            left = left[step:] - jnp.dot(
                (upper * pivots).T[at + step :],
                jnp.concatenate([upper, lower], axis=1),
                precision=HIGHEST,
                preferred_element_type=F32,
            )
    inverse = jnp.concatenate(inverse, axis=0)
    out[...] = jnp.dot(inverse, result[0], precision=HIGHEST, preferred_element_type=F32).T


def flip(rows, piece):
    piece[0] = rows[...].T


def touch(blocks, token):
    token[...] = jnp.zeros(token.shape, token.dtype)


def body(blocks, block_cols, counts, random_start_panel):
    counts = counts.reshape(-1)
    tiles = blocks[:, 0]
    (token,) = local(touch, [jax.ShapeDtypeStruct((8, 128), F32)], tiles)
    (piece,) = local(flip, [plain(1, BF)], random_start_panel)
    parts = gather_col(piece, token)
    for sweep in range(ITERS):
        image = reduce_row(*forward(block_cols, counts, tiles, parts))
        line = scatter_col(*backward(block_cols, counts, tiles, image))
        if sweep + 1 < ITERS:
            (piece,) = local(own_line, [plain(1, BF)], *line)
            parts = gather_col(piece)
    feature, width = line[0].shape[1:]
    result, gram = local(last_line, [plain(1), jax.ShapeDtypeStruct((feature, feature), F32)], *line)
    nodes = lax.axis_size("row") * lax.axis_size("col") * width

    def basis(*refs):
        basis_kernel(*refs, factor=math.sqrt(nodes))

    return local(basis, [jax.ShapeDtypeStruct((width, feature), F32)], all_sum(gram), result)[0]


def solution(mesh):
    return jax.shard_map(
        body,
        mesh=mesh,
        in_specs=(
            P("col", "row", None, None, None),
            P("col", "row", None),
            P("col", "row"),
            P(("row", "col"), None),
        ),
        out_specs=P(("row", "col"), None),
        check_vma=False,
    )
```

```python
import functools
import math

import jax
import jax.numpy as jnp
from jax import lax
from jax.experimental import pallas as pl
from jax.experimental.pallas import tpu as pltpu
from jax.sharding import PartitionSpec as P

ITERS = 2
CORE, ZLO, X = 1, 2, 8
Y, ZHI = 1, 4
DEAD = 32
TAIL = 16
STEPS = 32000.0
LEAST = 1e-30
BF, F32 = jnp.bfloat16, jnp.float32
HIGHEST = lax.Precision.HIGHEST


def swap(value, axis, bits):
    size = lax.axis_size(axis)
    return lax.ppermute(value, axis, [(i, i ^ bits) for i in range(size)])


def encode(*pairs):
    top = functools.reduce(jnp.maximum, [jnp.abs(part) for parts, _ in pairs for part in parts])
    top = jnp.maximum(jnp.max(top, axis=(0, 1), keepdims=True), LEAST)
    power = jnp.ceil(jnp.log2(top))
    scale = jnp.exp2(-power)
    for parts, ref in pairs:
        high, at = parts[0].shape[0], 0
        for part in parts:
            root = part * scale
            root = root * lax.rsqrt(jnp.abs(root) + LEAST)
            root = root * lax.rsqrt(jnp.abs(root) + LEAST)
            code = jnp.round(root * STEPS).astype(jnp.int32).astype(jnp.int16)
            for lane in range(0, part.shape[1], 128):
                ref[at : at + high] = code[:, lane : lane + 128]
                at += high
        ref[at:] = jnp.broadcast_to(power, (TAIL, 128)).astype(jnp.int32).astype(jnp.int16)


def decode(ref, high=128):
    count = (ref.shape[0] - TAIL) // (2 * high)
    gain = jnp.exp2(ref[2 * count * high :].astype(jnp.int32).astype(F32))[:1]
    parts = []
    for n in range(count):
        halves = []
        for at in (2 * n * high, (2 * n + 1) * high):
            root = ref[at : at + high].astype(jnp.int32).astype(F32) * (1.0 / STEPS)
            root = root * jnp.abs(root)
            halves.append(root * jnp.abs(root) * gain)
        parts.append(jnp.concatenate(halves, axis=1))
    return parts


def coded(count, feature=128):
    return jax.ShapeDtypeStruct((2 * count * feature + TAIL, 128), jnp.int16)


def plain(count, dtype=F32, feature=128, width=256):
    return jax.ShapeDtypeStruct((count, feature, width), dtype)


def local(kernel, outs, *args, scratch=(), limit=8):
    vmem = pl.BlockSpec(memory_space=pltpu.VMEM)
    return pl.pallas_call(
        kernel,
        in_specs=[vmem] * len(args),
        out_specs=[vmem] * len(outs),
        out_shape=outs,
        scratch_shapes=scratch,
        compiler_params=pltpu.CompilerParams(vmem_limit_bytes=limit << 20),
        cost_estimate=pl.CostEstimate(flops=1 << 20, bytes_accessed=1 << 20, transcendentals=0),
        name=kernel.__name__,
    )(*args)


def far_x(keep, other, low, high):
    two = [keep[8 + n] + other[n] for n in range(4)]
    encode((two[:2], low), (two[2:], high))


def near_x(keep, other, low, high, first, third):
    low, high = decode(low), decode(high)
    one = [keep[4 + n] + other[n] for n in range(4)]
    encode(([one[0] + low[0], one[1] + low[1], one[2], one[3]], first))
    three = [keep[12 + n] + other[4 + n] for n in range(4)]
    encode(([three[0], three[1], three[2] + high[0], three[3] + high[1]], third))


def own_x(keep, other, first, third, line, *far):
    first, third = decode(first), decode(third)
    total = [keep[n] + other[n] + (first[n] + third[n]) for n in range(4)]
    line[0] = total[0]
    encode(*(([total[n]], far[n - 1]) for n in (1, 2, 3)))


def own_line(line, one, two, three, piece):
    piece[0] = (line[0] + (decode(one)[0] + decode(two)[0] + decode(three)[0])).astype(BF)


def last_line(line, one, two, three, result, gram):
    total = line[0] + (decode(one)[0] + decode(two)[0] + decode(three)[0])
    result[0] = total
    gram[...] = lax.dot_general(
        total, total, (((1,), (1,)), ((), ())), precision=HIGHEST, preferred_element_type=F32
    )


def own_y(near, one, two, three, total, far):
    parts = [decode(ref) for ref in (one, two, three)]
    sums = [near[n] + (parts[0][n] + parts[1][n] + parts[2][n]) for n in (0, 1)]
    total[0], total[1] = sums
    encode((sums, far))


def own_row(total, far, image):
    far = decode(far)
    for n in (0, 1):
        image[n] = (total[n] + far[n]).astype(BF)


def join(a, b, c, d, *refs):
    for n, ref in enumerate((a, b, c, d)):
        refs[-1][n] = ref[0]


def gather_col(piece, *after):
    line = [piece] + [swap(piece, "col", ZLO * d) for d in (1, 2, 3)]
    (near,) = local(join, [plain(4, BF)], *line, *after)
    first, third = swap(near, "col", X * 1), swap(near, "col", X * 3)
    low, high = swap(first[:2], "col", X * 3), swap(third[2:], "col", X * 1)
    parts = [near, first, low, high, third]
    return parts + [swap(part, "col", CORE) for part in parts]


def scatter_col(keep, send2, send13, send0):
    two, rest, zero = (swap(part, "col", CORE) for part in (send2, send13, send0))
    low, high = local(far_x, [coded(2)] * 2, keep, two)
    low, high = swap(low, "col", X * 3), swap(high, "col", X * 1)
    first, third = local(near_x, [coded(4)] * 2, keep, rest, low, high)
    first, third = swap(first, "col", X * 1), swap(third, "col", X * 3)
    line, *far = local(own_x, [plain(1)] + [coded(1)] * 3, keep, zero, first, third)
    return [line] + [swap(far[d - 1], "col", ZLO * d) for d in (3, 2, 1)]


def reduce_row(near, *far):
    total, code = local(own_y, [plain(2), coded(2)], near, *far)
    (share,) = local(own_row, [plain(2, BF)], total, swap(code, "row", ZHI))
    one, three, two = (swap(share, "row", Y * d) for d in (1, 3, 2))
    return share, one, two, three


def slot_of(cols, counts, i, k):
    away = cols[i, 0, k] ^ lax.axis_index("col")
    return jnp.where(k < counts[i], (away % 2) * 16 + away // 2, DEAD)


def block_row(step):
    return step ^ (2 * (lax.axis_index("row") % 4))


def join_panel(near, first, third, near_other, first_other, third_other, panel):
    for at, own in ((0, (near, first, third)), (16, (near_other, first_other, third_other))):
        for distance, part in zip((0, 1, 3), own):
            panel[at + 4 * distance : at + 4 * distance + 4] = part[...]
    panel[DEAD] = jnp.zeros(panel.shape[1:], panel.dtype)


def image_rows(cols, counts, tiles, panel, step):
    i, total = block_row(step), None
    for k in range(tiles.shape[1]):
        part = lax.dot_general(
            panel[slot_of(cols, counts, i, k)], tiles[i, k], (((1,), (1,)), ((), ())), preferred_element_type=F32
        )
        total = part if total is None else total + part
    return total


def forward_far(cols, counts, tiles, before, low, high, low_other, high_other, one, two, three, panel):
    for at, part in ((8, low), (10, high), (24, low_other), (26, high_other)):
        panel[at : at + 2] = part[...]
    for distance, far in ((2, two), (1, one), (3, three)):
        encode(([image_rows(cols, counts, tiles, panel, 2 * distance + half) for half in (0, 1)], far))


def forward_near(cols, counts, tiles, panel, near):
    near[0] = image_rows(cols, counts, tiles, panel, 0)
    near[1] = image_rows(cols, counts, tiles, panel, 1)


def sweep_call(kernel, quarter, cols, counts, tiles, operands, outs, aliases=()):
    vmem, smem = pl.BlockSpec(memory_space=pltpu.VMEM), pl.BlockSpec(memory_space=pltpu.SMEM)
    return pl.pallas_call(
        kernel,
        in_specs=[smem, smem] + [vmem] * (1 + len(operands)),
        out_specs=[vmem] * len(outs),
        out_shape=outs,
        input_output_aliases=dict(aliases),
        compiler_params=pltpu.CompilerParams(vmem_limit_bytes=8 << 20),
        cost_estimate=pl.CostEstimate(
            flops=quarter * 32 * 256 * 256 * 128, bytes_accessed=quarter << 20, transcendentals=0
        ),
        name=kernel.__name__,
    )(cols, counts, tiles, *operands)


def forward(cols, counts, tiles, parts):
    near, first, low, high, third = parts[:5]
    others = parts[5:]
    (panel,) = local(join_panel, [plain(DEAD + 1, BF)], near, first, third, others[0], others[1], others[4])
    outs = [coded(2)] * 3 + [plain(DEAD + 1, BF)]
    *far, panel = sweep_call(
        forward_far, 3, cols, counts, tiles, [panel, low, high, others[2], others[3]], outs, [(3, 3)]
    )
    far = [swap(far[d - 1], "row", Y * d) for d in (1, 3, 2)]
    (near,) = sweep_call(forward_near, 1, cols, counts, tiles, [panel], [plain(2)])
    return near, *far


def add_rows(cols, counts, tiles, image, total, distance):
    for half in (0, 1):
        i = block_row(2 * distance + half)
        for k in range(tiles.shape[1]):
            total[slot_of(cols, counts, i, k)] += jnp.dot(image[half], tiles[i, k], preferred_element_type=F32)


def backward_near(cols, counts, tiles, image, total):
    total[...] = jnp.zeros(total.shape, total.dtype)
    add_rows(cols, counts, tiles, image, total, 0)


def backward_three(cols, counts, tiles, before, image, total):
    add_rows(cols, counts, tiles, image, total, 3)


def backward_one(cols, counts, tiles, before, image, total):
    add_rows(cols, counts, tiles, image, total, 1)


def backward_two(cols, counts, tiles, before, image, keep, send2, send13, send0, total):
    add_rows(cols, counts, tiles, image, total, 2)
    keep[...] = total[0:16]
    send0[...] = total[16:20]
    send13[0:4] = total[20:24]
    send2[...] = total[24:28]
    send13[4:8] = total[28:32]


def backward(cols, counts, tiles, image):
    whole = plain(DEAD + 1)
    (total,) = sweep_call(backward_near, 1, cols, counts, tiles, [image[0]], [whole])
    (total,) = sweep_call(backward_one, 1, cols, counts, tiles, [total, image[1]], [whole], [(3, 0)])
    (total,) = sweep_call(backward_three, 1, cols, counts, tiles, [total, image[3]], [whole], [(3, 0)])
    outs = [plain(16), plain(4), plain(8), plain(4), whole]
    return sweep_call(backward_two, 1, cols, counts, tiles, [total, image[2]], outs, [(3, 4)])[:4]


def all_sum(total):
    total = total + swap(total, "col", CORE)
    for axis, bits, order in (("col", X, (2, 3, 1)), ("col", ZLO, (1, 2, 3)), ("row", Y, (2, 3, 1))):
        got = [swap(total, axis, bits * d) for d in order]
        total = (got[0] + got[1]) + (got[2] + total)
    return total + swap(total, "row", ZHI)


def basis_kernel(gram, result, out, *, factor):
    n, step = gram.shape[0], 32
    row = lax.broadcasted_iota(jnp.int32, (n, n), 0)
    lane = lax.broadcasted_iota(jnp.int32, (n, n), 1)
    left = jnp.concatenate([gram[...], jnp.where(row == lane, 1.0, 0.0)], axis=1)
    row, inverse = row[:step], []
    for at in range(0, n, step):
        upper, lower = left[:step, :n], left[:step, n:]
        columns = [jnp.broadcast_to(upper[:, at + c : at + c + 1], (step, n)) for c in range(step)]
        pivots = jnp.zeros((step, n), F32)
        for j in range(step):
            pivot = 1.0 / columns[j][j : j + 1]
            ratio = jnp.where(row > j, columns[j] * pivot, 0.0)
            for c in range(j + 1, step):
                columns[c] = columns[c] - ratio * columns[c][j : j + 1]
            upper = upper - ratio * upper[j : j + 1]
            lower = lower - ratio * lower[j : j + 1]
            pivots = jnp.where(row == j, pivot, pivots)
        inverse.append(lower * (jnp.sqrt(pivots) * factor))
        if at + step < n:
            left = left[step:] - jnp.dot(
                (upper * pivots).T[at + step :],
                jnp.concatenate([upper, lower], axis=1),
                precision=HIGHEST,
                preferred_element_type=F32,
            )
    inverse = jnp.concatenate(inverse, axis=0)
    out[...] = jnp.dot(inverse, result[0], precision=HIGHEST, preferred_element_type=F32).T


def flip(rows, piece):
    piece[0] = rows[...].T


def touch(blocks, token):
    token[...] = jnp.zeros(token.shape, token.dtype)


def body(blocks, block_cols, counts, random_start_panel):
    counts = counts.reshape(-1)
    tiles = blocks[:, 0]
    (token,) = local(touch, [jax.ShapeDtypeStruct((8, 128), F32)], tiles)
    (piece,) = local(flip, [plain(1, BF)], random_start_panel)
    parts = gather_col(piece, token)
    for sweep in range(ITERS):
        image = reduce_row(*forward(block_cols, counts, tiles, parts))
        line = scatter_col(*backward(block_cols, counts, tiles, image))
        if sweep + 1 < ITERS:
            (piece,) = local(own_line, [plain(1, BF)], *line)
            parts = gather_col(piece)
    feature, width = line[0].shape[1:]
    result, gram = local(last_line, [plain(1), jax.ShapeDtypeStruct((feature, feature), F32)], *line)
    nodes = lax.axis_size("row") * lax.axis_size("col") * width

    def basis(*refs):
        basis_kernel(*refs, factor=math.sqrt(nodes))

    return local(basis, [jax.ShapeDtypeStruct((width, feature), F32)], all_sum(gram), result)[0]


def solution(mesh):
    return jax.shard_map(
        body,
        mesh=mesh,
        in_specs=(
            P("col", "row", None, None, None),
            P("col", "row", None),
            P("col", "row"),
            P(("row", "col"), None),
        ),
        out_specs=P(("row", "col"), None),
        check_vma=False,
    )
```
